32 devices in a mesh: term: 4 (over z), doc: 8 (over y, x, core).
Axes of the slice: x: 2, y: 2, z: 4, core: 2. Of those that a mesh axis runs over, the one named last changes fastest.
Arguments:
- postings: bfloat16 [4096, 30720], P('doc', 'term'), may hold values from 0 to 3
- query_terms: int32 [128, 32], replicated, may hold values from 0 to 30719
- query_levels: int32 [128, 32], replicated, may hold values from 1 to 255
- feedback_ids: int32 [128, 10], replicated, may hold values from 0 to 4095, as said below
Outputs:
- first_scores: float32 [128, 4096], P('term', 'doc')
- final_scores: float32 [128, 4096], P('term', 'doc')
The draws below stay inside these ranges and needn't reach their ends.
Inputs may be any that keep to these rules, and one draw needn't show every extreme that they name: `feedback_ids`: the 1280 feedback ids are all different.
All inputs are finite; a program needn't handle non-finite values.
Results may differ from the reference program's by a relative error of at most 0.0015.
Values may be sent and summed in bfloat16 or wider, within the bound.
A program may use at most 64 MiB of HBM per device.

```python
import math
import jax
import jax.numpy as jnp
from jax import lax

VOCAB = 30720
Q = 128
QT = 32
FB = 10
TOPICS = 256
DOCS = 4096


background_share = 0.004


def topic_tables(key):
    term_order = jax.random.permutation(jax.random.fold_in(key, 101), VOCAB).astype(jnp.int32)
    term_positions = jnp.arange(VOCAB, dtype=jnp.int32)
    term_topic = jnp.zeros((VOCAB,), jnp.int32).at[term_order].set(term_positions % TOPICS)
    query_topic = jax.random.randint(jax.random.fold_in(key, 102), (Q,), 0, TOPICS, dtype=jnp.int32)
    shuffled = jax.random.permutation(jax.random.fold_in(key, 103), DOCS).astype(jnp.int32)
    at_ends = (shuffled == 0) | (shuffled == DOCS - 1)
    rank_keys = jnp.where(at_ends, -1, jnp.arange(DOCS, dtype=jnp.int32))
    picked = shuffled[jnp.argsort(rank_keys, stable=True)][:Q * FB]
    picked = jax.random.permutation(jax.random.fold_in(key, 104), picked)
    feedback_ids = picked.reshape(Q, FB)
    base_topic = jax.random.randint(jax.random.fold_in(key, 105), (DOCS,), 0, TOPICS, dtype=jnp.int32)
    passage_topic = base_topic.at[picked].set(jnp.repeat(query_topic, FB))
    return (term_order, term_topic, query_topic, feedback_ids, passage_topic)


def draw_postings(key, part):
    term_order, term_topic, query_topic, feedback_ids, passage_topic = topic_tables(key)
    uniform_draw = jax.random.uniform(jax.random.fold_in(key, 106), (DOCS, VOCAB), jnp.float32)
    core_mask = passage_topic[:, None] == term_topic[None, :]
    spare_mask = uniform_draw < background_share
    spare_level = uniform_draw / background_share
    core_value = 0.1 * jnp.exp(uniform_draw * math.log(30.0))
    spare_value = 0.02 * jnp.exp(spare_level * math.log(50.0))
    weights = jnp.where(core_mask, core_value, jnp.where(spare_mask, spare_value, 0.0))
    return weights.astype(jnp.bfloat16)


def draw_query_terms(key, part):
    term_order, term_topic, query_topic, feedback_ids, passage_topic = topic_tables(key)
    core_slots = QT // 2
    slot_picks = jax.random.randint(jax.random.fold_in(key, 107), (Q, core_slots), 0, VOCAB // TOPICS, dtype=jnp.int32)
    core_terms = term_order[query_topic[:, None] + TOPICS * slot_picks]
    other_terms = jax.random.randint(jax.random.fold_in(key, 108), (Q, QT - core_slots), 0, VOCAB, dtype=jnp.int32)
    low_row = jax.random.randint(jax.random.fold_in(key, 109), (), 0, Q, dtype=jnp.int32)
    high_row = jax.random.randint(jax.random.fold_in(key, 110), (), 0, Q, dtype=jnp.int32)
    other_terms = other_terms.at[low_row, 0].set(0).at[high_row, 1].set(VOCAB - 1)
    all_slots = jnp.concatenate([core_terms, other_terms], axis=1)
    return jax.random.permutation(jax.random.fold_in(key, 111), all_slots, axis=1, independent=True)


def draw_feedback_ids(key, part):
    term_order, term_topic, query_topic, feedback_ids, passage_topic = topic_tables(key)
    return feedback_ids


def touch_ends(values, stream_key, smallest, top_value):
    spot = [jax.random.randint(jax.random.fold_in(stream_key, axis), (), 0, length) for axis, length in enumerate(values.shape)]
    longest = values.shape.index(max(values.shape))
    next_to = spot[:longest] + [(spot[longest] + 1) % values.shape[longest]] + spot[longest + 1:]
    return values.at[tuple(spot)].set(smallest).at[tuple(next_to)].set(top_value)


def setup_inputs(seed: int = 0) -> dict:
    streams_of = jax.random.split(jax.random.key(seed), 5)
    return {
        "postings": draw_postings(jax.random.fold_in(streams_of[4], 71), 0),
        "query_terms": draw_query_terms(jax.random.fold_in(streams_of[4], 71), 0),
        "query_levels": touch_ends(jax.random.randint(streams_of[2], (Q, QT), 1, 256), jax.random.fold_in(streams_of[2], 1), 1, 255).astype(jnp.int32),
        "feedback_ids": draw_feedback_ids(jax.random.fold_in(streams_of[4], 71), 0),
    }


expansion_weight = 0.25


def score_all(query_rows, postings):
    return lax.dot_general(query_rows, postings, (((1,), (1,)), ((), ())), preferred_element_type=jnp.float32)


def reference(postings, query_terms, query_levels, feedback_ids):
    queries = query_terms.shape[0]
    row_index = jnp.broadcast_to(jnp.arange(queries, dtype=jnp.int32)[:, None], query_terms.shape)
    query_vector = jnp.zeros((queries, VOCAB), jnp.float32).at[row_index, query_terms].add(query_levels.astype(jnp.float32) / 100.0)
    first_scores = score_all(query_vector.astype(jnp.bfloat16), postings)
    feedback = jnp.take_along_axis(first_scores, feedback_ids, axis=1).astype(jnp.bfloat16)
    feedback_rows = jnp.broadcast_to(jnp.arange(queries, dtype=jnp.int32)[:, None], feedback_ids.shape)
    mixing = jnp.zeros((queries, DOCS), jnp.float32).at[feedback_rows, feedback_ids].add(feedback.astype(jnp.float32)).astype(jnp.bfloat16)
    numerator = jnp.dot(mixing, postings, preferred_element_type=jnp.float32)
    weight_sum = jnp.sum(feedback.astype(jnp.float32), axis=1)
    expanded = (query_vector + expansion_weight * numerator / weight_sum[:, None]).astype(jnp.bfloat16)
    final_scores = score_all(expanded, postings)
    return first_scores, final_scores
```

```python
import functools

import jax
import jax.numpy as jnp
from jax import lax
from jax.experimental import pallas as pl
from jax.experimental.pallas import tpu as pltpu
from jax.sharding import PartitionSpec as P

expansion_weight = 0.25
MESH = pl.DeviceIdType.MESH
LANES = 128
NT = (((1,), (1,)), ((), ()))
f32 = jnp.float32
bf16 = jnp.bfloat16


def dot_nt(a, b):
    return lax.dot_general(a, b, NT, preferred_element_type=f32)


def fused_kernel(
    n_term, n_doc, chunks,
    postings, terms, levels, ids, first_out, final_out,
    p_ref, q_ref, hi_ref, lo_ref, lev_ref, part_ref, sel_ref, mix_ref,
    fb_ref, first_ref, ws_ref, wcol_ref, nb_ref, tw_ref, s1_ref, a_ref, s2_ref, b_ref,
    e_ref, acc_ref, last_ref,
    p_sem, fb_send, fb_recv, first_send, first_recv, ws_send, ws_recv,
    pipe_send, pipe_recv, last_send, last_recv,
):
    t = lax.axis_index("term")
    d = lax.axis_index("doc")
    docs, width = p_ref.shape
    queries, slots = terms.shape
    cw = width // chunks
    his = width // LANES
    rows_out = queries // n_term
    half, quarter, eighth = queries // 2, queries // 4, queries // 8

    core = d % 2
    bit1 = (d // 2) % 2
    bit2 = (d // 4) % 2

    def cols(c):
        return pl.ds(pl.multiple_of(c * cw, LANES), cw)

    def load(c):
        return pltpu.make_async_copy(postings.at[:, cols(c)], p_ref.at[:, cols(c)], p_sem.at[c])

    for c in range(chunks):
        load(c).start()

    barrier = pltpu.get_barrier_semaphore()
    for o in range(1, n_term):
        pl.semaphore_signal(barrier, inc=1, device_id={"term": (t + o) % n_term}, device_id_type=MESH)
    for o in range(1, n_doc):
        pl.semaphore_signal(barrier, inc=1, device_id={"doc": (d + o) % n_doc}, device_id_type=MESH)

    group = 8 * slots
    spread = (
        lax.broadcasted_iota(jnp.int32, (slots, group), 0)
        == lax.broadcasted_iota(jnp.int32, (slots, group), 1) % slots
    ).astype(bf16)
    own = (
        lax.broadcasted_iota(jnp.int32, (queries, group), 0) % 8
        == lax.broadcasted_iota(jnp.int32, (queries, group), 1) // slots
    )

    def lay(values):
        wide = jnp.dot(values.astype(f32).astype(bf16), spread, preferred_element_type=f32)
        return jnp.sum(jnp.where(own, wide, 0.0).reshape(queries // 8, 8, group), axis=1)

    ids_now = terms[...]
    q8 = (lax.broadcasted_iota(jnp.int32, (queries // 8, group), 1) // slots).astype(f32)
    hi = lay(ids_now // LANES) - (t * his).astype(f32)
    hi_ref[...] = hi * 8.0 + q8
    lo_ref[...] = lay(ids_now % LANES)
    lev_ref[...] = lay(levels[...])

    row_code = lax.broadcasted_iota(jnp.int32, (his * 8, group), 0).astype(f32)
    lane_code = lax.broadcasted_iota(jnp.int32, (LANES, group), 0).astype(f32)

    def build(g, carry):
        left = jnp.where(
            hi_ref[pl.ds(g, 1), :] == row_code, lev_ref[pl.ds(g, 1), :], 0.0
        ).astype(bf16)
        right = jnp.where(lo_ref[pl.ds(g, 1), :] == lane_code, 1.0, 0.0).astype(bf16)
        block = dot_nt(left, right) * 0.01
        rows = pl.ds(pl.multiple_of(g * 8, 8), 8)
        for h in range(his):
            q_ref[rows, h * LANES : (h + 1) * LANES] = block[h * 8 : (h + 1) * 8]
        return carry

    lax.fori_loop(0, queries // 8, build, 0)

    place = lax.broadcasted_iota(jnp.int32, (queries, docs), 1)
    local = ids[...] - d * docs
    sel = place == local[:, 0:1]
    for j in range(1, local.shape[1]):
        sel = sel | (place == local[:, j : j + 1])
    sel_ref[...] = jnp.where(sel, 1.0, 0.0)

    part_ref[...] = jnp.zeros_like(part_ref)

    def score(c, carry):
        load(c).wait()
        part_ref[...] += dot_nt(q_ref[:, cols(c)].astype(bf16), p_ref[:, cols(c)])
        return carry

    lax.fori_loop(0, chunks, score, 0)

    pl.semaphore_wait(barrier, n_term + n_doc - 2)

    fb_ref[t] = jnp.sum((sel_ref[...] * part_ref[...]).reshape(queries // 8, 8, docs), axis=0)

    def fb_copy(o):
        return pltpu.make_async_remote_copy(
            fb_ref.at[t], fb_ref.at[t], fb_send.at[o - 1], fb_recv.at[o - 1],
            device_id={"term": (t + o) % n_term}, device_id_type=MESH,
        )

    def first_copy(o):
        peer = (t + o) % n_term
        return pltpu.make_async_remote_copy(
            part_ref.at[pl.ds(pl.multiple_of(peer * rows_out, 8), rows_out), :], first_ref.at[t],
            first_send.at[o - 1], first_recv.at[o - 1],
            device_id={"term": peer}, device_id_type=MESH,
        )

    def last_copy(o):
        peer = (t + o) % n_term
        return pltpu.make_async_remote_copy(
            acc_ref.at[pl.ds(pl.multiple_of(peer * rows_out, 8), rows_out), :], last_ref.at[t],
            last_send.at[o - 1], last_recv.at[o - 1],
            device_id={"term": peer}, device_id_type=MESH,
        )

    def ws_copy(o):
        return pltpu.make_async_remote_copy(
            ws_ref.at[d], ws_ref.at[d], ws_send.at[o - 1], ws_recv.at[o - 1],
            device_id={"doc": (d + o) % n_doc}, device_id_type=MESH,
        )

    for o in range(1, n_term):
        fb_copy(o).start()
    for o in range(1, n_term):
        first_copy(o).start()
    own_rows = pl.ds(pl.multiple_of(t * rows_out, 8), rows_out)
    first_ref[t] = part_ref[own_rows, :]
    for o in range(1, n_term):
        fb_copy(o).wait_recv()
    fb_sum = fb_ref[0]
    for s in range(1, n_term):
        fb_sum = fb_sum + fb_ref[s]
    fb_row = jnp.sum(fb_sum, axis=0, keepdims=True)
    mix_ref[...] = (sel_ref[...] * fb_row).astype(bf16)

    ones = jnp.ones((16, docs), bf16)
    ws_ref[d] = dot_nt(ones, mix_ref[...])[:8]
    for o in range(1, n_doc):
        ws_copy(o).start()

    def copy_of(step, c, src, dst, peer):
        return pltpu.make_async_remote_copy(
            src, dst, pipe_send.at[step, c], pipe_recv.at[step, c],
            device_id={"doc": peer}, device_id_type=MESH,
        )

    twin = d + 1 - 2 * core

    def way(c):
        odd = c % 2
        even = 1 - odd
        in1 = even * bit1 + odd * bit2
        in2 = even * bit2 + odd * bit1
        peer1 = d + (even * 2 + odd * 4) * (1 - 2 * in1)
        peer2 = d + (even * 4 + odd * 2) * (1 - 2 * in2)
        return in1, in2, peer1, peer2

    def rows(start, size):
        return pl.ds(pl.multiple_of(start, 16), size)

    def exchange(step, c):
        in1, in2, peer1, peer2 = way(c)
        here = cols(c)
        if step == 0:
            return copy_of(0, c, nb_ref.at[rows((1 - core) * half, half), here], tw_ref.at[:, here], twin)
        if step == 1:
            return copy_of(1, c, s1_ref.at[rows((1 - in1) * quarter, quarter), here], a_ref.at[:, here], peer1)
        if step == 2:
            return copy_of(2, c, s2_ref.at[rows((1 - in2) * eighth, eighth), here], b_ref.at[:, here], peer2)
        base = core * half
        if step == 3:
            at = e_ref.at[rows(base + in1 * quarter + in2 * eighth, eighth), here]
            return copy_of(3, c, at, at, peer2)
        if step == 4:
            at = e_ref.at[rows(base + in1 * quarter, quarter), here]
            return copy_of(4, c, at, at, peer1)
        at = e_ref.at[rows(base, half), here]
        return copy_of(5, c, at, at, twin)

    acc_ref[...] = jnp.zeros_like(acc_ref)

    def stage(step, s, body):
        c = s - step

        @pl.when((c >= 0) & (c < chunks))
        def _():
            body(c)

    def step1(c):
        exchange(0, c).wait_recv()
        here = cols(c)
        s1_ref[:, here] = (
            nb_ref[rows(core * half, half), here].astype(f32) + tw_ref[:, here].astype(f32)
        ).astype(bf16)
        exchange(1, c).start()

    def step2(c):
        in1, in2, _, _ = way(c)
        exchange(1, c).wait_recv()
        here = cols(c)
        s2_ref[:, here] = (
            s1_ref[rows(in1 * quarter, quarter), here].astype(f32) + a_ref[:, here].astype(f32)
        ).astype(bf16)
        exchange(2, c).start()

    def step3(c):
        in1, in2, _, _ = way(c)
        exchange(2, c).wait_recv()
        here = cols(c)
        numerator = s2_ref[rows(in2 * eighth, eighth), here].astype(f32) + b_ref[:, here].astype(f32)
        mine = rows(core * half + in1 * quarter + in2 * eighth, eighth)
        total = wcol_ref[mine, :][:, 0:1]
        e_ref[mine, here] = (q_ref[mine, here] + expansion_weight * numerator / total).astype(bf16)
        exchange(3, c).start()

    def step4(c):
        exchange(3, c).wait_recv()
        exchange(4, c).start()

    def step5(c):
        exchange(4, c).wait_recv()
        exchange(5, c).start()

    def step0(c):
        here = cols(c)
        nb_ref[:, here] = jnp.dot(mix_ref[...], p_ref[:, here], preferred_element_type=f32).astype(bf16)
        exchange(0, c).start()

    def step6(c):
        exchange(5, c).wait_recv()
        here = cols(c)
        acc_ref[...] += dot_nt(e_ref[:, here], p_ref[:, here])

    def pipeline(s, carry):
        @pl.when(s == 3)
        def _():
            for o in range(1, n_doc):
                ws_copy(o).wait_recv()
            total = ws_ref[0]
            for o in range(1, n_doc):
                total = total + ws_ref[o]
            shape = (queries, queries)
            eye = lax.broadcasted_iota(jnp.int32, shape, 0) == lax.broadcasted_iota(jnp.int32, shape, 1)
            column = jnp.sum(jnp.where(eye, total[0:1, :], 0.0), axis=1, keepdims=True)
            wcol_ref[...] = jnp.broadcast_to(column, wcol_ref.shape)

        stage(5, s, step5)
        stage(4, s, step4)
        stage(3, s, step3)
        stage(2, s, step2)
        stage(1, s, step1)
        stage(0, s, step0)
        stage(6, s, step6)
        return carry

    lax.fori_loop(0, chunks + 6, pipeline, 0)

    for o in range(1, n_term):
        last_copy(o).start()

    for o in range(1, n_term):
        first_copy(o).wait_recv()
    total = first_ref[0]
    for s in range(1, n_term):
        total = total + first_ref[s]
    first_out[...] = total

    last_ref[t] = acc_ref[own_rows, :]
    for o in range(1, n_term):
        last_copy(o).wait_recv()
    total = last_ref[0]
    for s in range(1, n_term):
        total = total + last_ref[s]
    final_out[...] = total

    for o in range(1, n_term):
        fb_copy(o).wait_send()
        first_copy(o).wait_send()
        last_copy(o).wait_send()
    for o in range(1, n_doc):
        ws_copy(o).wait_send()

    def drain(c, carry):
        for step in range(6):
            exchange(step, c).wait_send()
        return carry

    lax.fori_loop(0, chunks, drain, 0)


def fused(postings, query_terms, query_levels, feedback_ids):
    docs, width = postings.shape
    queries, slots = query_terms.shape
    n_term, n_doc = lax.axis_size("term"), lax.axis_size("doc")
    chunks = next(c for c in (6, 4, 2, 1) if width % (c * LANES) == 0)
    rows_out = queries // n_term
    group = 8 * slots
    vmem = pltpu.VMEM
    dma = pltpu.SemaphoreType.DMA
    out = jax.ShapeDtypeStruct((rows_out, docs), f32)
    return pl.pallas_call(
        functools.partial(fused_kernel, n_term, n_doc, chunks),
        out_shape=(out, out),
        in_specs=[pl.BlockSpec(memory_space=pl.ANY)] + [pl.BlockSpec(memory_space=pltpu.VMEM)] * 3,
        out_specs=(pl.BlockSpec(memory_space=pltpu.VMEM),) * 2,
        scratch_shapes=[
            vmem((docs, width), bf16),
            vmem((queries, width), f32),
            vmem((queries // 8, group), f32),
            vmem((queries // 8, group), f32),
            vmem((queries // 8, group), f32),
            vmem((queries, docs), f32),
            vmem((queries, docs), f32),
            vmem((queries, docs), bf16),
            vmem((n_term, 8, docs), f32),
            vmem((n_term, rows_out, docs), f32),
            vmem((n_doc, 8, queries), f32),
            vmem((queries, LANES), f32),
            vmem((queries, width), bf16),
            vmem((queries // 2, width), bf16),
            vmem((queries // 2, width), bf16),
            vmem((queries // 4, width), bf16),
            vmem((queries // 4, width), bf16),
            vmem((queries // 8, width), bf16),
            vmem((queries, width), bf16),
            vmem((queries, docs), f32),
            vmem((n_term, rows_out, docs), f32),
            dma((chunks,)),
            dma((n_term - 1,)),
            dma((n_term - 1,)),
            dma((n_term - 1,)),
            dma((n_term - 1,)),
            dma((n_doc - 1,)),
            dma((n_doc - 1,)),
            dma((6, chunks)),
            dma((6, chunks)),
            dma((n_term - 1,)),
            dma((n_term - 1,)),
        ],
        compiler_params=pltpu.CompilerParams(
            collective_id=0, has_side_effects=True, vmem_limit_bytes=48 * 1024 * 1024
        ),
        cost_estimate=pl.CostEstimate(
            flops=6 * queries * docs * width, bytes_accessed=2 * docs * width, transcendentals=0
        ),
        name="fused_feedback",
    )(postings, query_terms, query_levels, feedback_ids)


def query_slice(query_terms, query_levels, width, offset):
    columns = offset + lax.iota(jnp.int32, width)

    def add_term(position, total):
        ids_now = lax.dynamic_index_in_dim(query_terms, position, 1, keepdims=True)
        weight_now = (
            lax.dynamic_index_in_dim(query_levels, position, 1, keepdims=True).astype(f32) / 100.0
        )
        return total + jnp.where(ids_now == columns[None, :], weight_now, 0.0)

    initial = jnp.zeros((query_terms.shape[0], width), f32)
    return lax.fori_loop(0, query_terms.shape[1], add_term, initial)


def general(postings, query_terms, query_levels, feedback_ids):
    doc_rows, width = postings.shape
    queries = query_terms.shape[0]
    group_rows = queries // lax.axis_size("term")
    term_index = lax.axis_index("term")
    doc_index = lax.axis_index("doc")
    query_part = query_slice(query_terms, query_levels, width, term_index * width)
    local_slot = feedback_ids - doc_index * doc_rows
    positions = lax.iota(jnp.int32, doc_rows)
    selector = (local_slot[:, :, None] == positions[None, None, :]).astype(f32)
    first_all = lax.psum(dot_nt(query_part.astype(bf16), postings), "term")
    first_scores = lax.dynamic_slice_in_dim(first_all, term_index * group_rows, group_rows, 0)
    feedback = jnp.sum(selector * first_all[:, None, :], axis=2).astype(bf16).astype(f32)
    mixing = jnp.sum(selector * feedback[:, :, None], axis=1).astype(bf16)
    numerator = jnp.dot(mixing, postings, preferred_element_type=f32)
    numerator, weight_sum = lax.psum((numerator, jnp.sum(feedback, axis=1)), "doc")
    expanded = (query_part + expansion_weight * numerator / weight_sum[:, None]).astype(bf16)
    final_scores = lax.psum_scatter(
        dot_nt(expanded, postings), "term", scatter_dimension=0, tiled=True
    )
    return first_scores, final_scores


def per_device(postings, query_terms, query_levels, feedback_ids):
    docs, width = postings.shape
    queries, slots = query_terms.shape
    fits = (
        lax.axis_size("doc") == 8
        and lax.axis_size("term") > 1
        and queries == LANES
        and queries % (8 * lax.axis_size("term")) == 0
        and width % LANES == 0
        and docs % LANES == 0
    )
    run = fused if fits else general
    return run(postings, query_terms, query_levels, feedback_ids)


def solution(mesh):
    return jax.shard_map(
        per_device,
        mesh=mesh,
        in_specs=(P("doc", "term"), P(), P(), P()),
        out_specs=(P("term", "doc"), P("term", "doc")),
        check_vma=False,
    )
```

```python
import functools

import jax
import jax.numpy as jnp
from jax import lax
from jax.experimental import pallas as pl
from jax.experimental.pallas import tpu as pltpu
from jax.sharding import PartitionSpec as P

expansion_weight = 0.25
MESH = pl.DeviceIdType.MESH
LANES = 128
NT = (((1,), (1,)), ((), ()))
f32 = jnp.float32
bf16 = jnp.bfloat16


def dot_nt(a, b):
    return lax.dot_general(a, b, NT, preferred_element_type=f32)


def plan(chunks, mega):
    part = mega / chunks
    send = (part * 0.83, part * 5.0, part * 2.5, part * 2.5, part * 5.0, part * 0.83)
    work = (3.0 / chunks, 1.0 / chunks, 0.5 / chunks, 1.0 / chunks, 0.02, 0.02, 4.0 / chunks)
    free = {"twin": 0.0, "x": 0.0, "y": 0.0}
    arrival, at, order = {}, [0] * 7, []
    now = 0.0
    rank = (5, 4, 3, 2, 1, 0, 6)

    def due(k):
        return 0.0 if k == 0 else arrival.get((k - 1, at[k]), float("inf"))

    while at[6] < chunks:
        open_steps = [k for k in rank if at[k] < chunks]
        ready = [k for k in open_steps if due(k) <= now]
        k = ready[0] if ready else min(open_steps, key=due)
        c = at[k]
        now = max(now, due(k)) + work[k]
        if k < 6:
            link = "twin" if k in (0, 5) else "xy"[(c + (k in (2, 3))) % 2]
            free[link] = max(now, free[link]) + send[k]
            arrival[k, c] = free[link] + 1.0
        at[k] += 1
        order.append((k, c))
    return order


def fused_kernel(
    n_term, n_doc, chunks, loads,
    postings, terms, levels, ids, first_out, final_out,
    p_ref, q_ref, hi_ref, lo_ref, lev_ref, part_ref, sel_ref, mix_ref,
    fb_ref, first_ref, ws_ref, wcol_ref, nb_ref, tw_ref, s1_ref, a_ref, s2_ref, b_ref,
    e_ref, acc_ref, code_ref, last_ref, top_ref, tops_ref,
    p_sem, fb_send, fb_recv, first_send, first_recv, ws_send, ws_recv,
    pipe_send, pipe_recv, last_send, last_recv, top_send, top_recv,
):
    t = lax.axis_index("term")
    d = lax.axis_index("doc")
    docs, width = p_ref.shape
    slots, queries = terms.shape
    cw = width // chunks
    lw = width // loads
    his = width // LANES
    rows_out = queries // n_term
    half, quarter, eighth = queries // 2, queries // 4, queries // 8

    core = d % 2
    bit1 = (d // 2) % 2
    bit2 = (d // 4) % 2

    def cols(c):
        return pl.ds(pl.multiple_of(c * cw, LANES), cw)

    def load_cols(c):
        return pl.ds(pl.multiple_of(c * lw, LANES), lw)

    def load(c):
        here = load_cols(c)
        return pltpu.make_async_copy(postings.at[:, here], p_ref.at[:, here], p_sem.at[c])

    for c in range(loads):
        load(c).start()

    barrier = pltpu.get_barrier_semaphore()
    for o in range(1, n_term):
        pl.semaphore_signal(barrier, inc=1, device_id={"term": (t + o) % n_term}, device_id_type=MESH)
    for o in range(1, n_doc):
        pl.semaphore_signal(barrier, inc=1, device_id={"doc": (d + o) % n_doc}, device_id_type=MESH)

    group = 8 * slots
    spread = (
        lax.broadcasted_iota(jnp.int32, (slots, group), 0)
        == lax.broadcasted_iota(jnp.int32, (slots, group), 1) % slots
    ).astype(bf16)
    own = (
        lax.broadcasted_iota(jnp.int32, (queries, group), 0) % 8
        == lax.broadcasted_iota(jnp.int32, (queries, group), 1) // slots
    )

    def lay(values):
        wide = lax.dot_general(
            values.astype(f32).astype(bf16), spread, (((0,), (0,)), ((), ())), preferred_element_type=f32
        )
        return jnp.sum(jnp.where(own, wide, 0.0).reshape(queries // 8, 8, group), axis=1)

    ids_now = terms[...]
    q8 = (lax.broadcasted_iota(jnp.int32, (queries // 8, group), 1) // slots).astype(f32)
    hi = lay(ids_now // LANES) - (t * his).astype(f32)
    hi_ref[...] = hi * 8.0 + q8
    lo_ref[...] = lay(ids_now % LANES)
    lev_ref[...] = lay(levels[...])

    row_code = lax.broadcasted_iota(jnp.int32, (his * 8, group), 0).astype(f32)
    lane_code = lax.broadcasted_iota(jnp.int32, (LANES, group), 0).astype(f32)

    def build_one(g):
        left = jnp.where(
            hi_ref[pl.ds(g, 1), :] == row_code, lev_ref[pl.ds(g, 1), :], 0.0
        ).astype(bf16)
        right = jnp.where(lo_ref[pl.ds(g, 1), :] == lane_code, 1.0, 0.0).astype(bf16)
        block = dot_nt(left, right) * 0.01
        rows = pl.ds(pl.multiple_of(g * 8, 8), 8)
        for h in range(his):
            q_ref[rows, h * LANES : (h + 1) * LANES] = block[h * 8 : (h + 1) * 8]

    def build(g, carry):
        for i in range(4):
            build_one(g * 4 + i)
        return carry

    lax.fori_loop(0, queries // 32, build, 0)

    place = lax.broadcasted_iota(jnp.int32, (queries, docs), 1)
    local = ids[...].T - d * docs
    sel = place == local[:, 0:1]
    for j in range(1, local.shape[1]):
        sel = sel | (place == local[:, j : j + 1])
    sel_ref[...] = jnp.where(sel, 1.0, 0.0)

    part_ref[...] = jnp.zeros_like(part_ref)

    def score(c, carry):
        load(c).wait()
        part_ref[...] += dot_nt(q_ref[:, load_cols(c)].astype(bf16), p_ref[:, load_cols(c)])
        return carry

    lax.fori_loop(0, loads, score, 0)

    pl.semaphore_wait(barrier, n_term + n_doc - 2)

    fb_ref[t] = jnp.sum((sel_ref[...] * part_ref[...]).reshape(queries // 8, 8, docs), axis=0)

    def fb_copy(o):
        return pltpu.make_async_remote_copy(
            fb_ref.at[t], fb_ref.at[t], fb_send.at[o - 1], fb_recv.at[o - 1],
            device_id={"term": (t + o) % n_term}, device_id_type=MESH,
        )

    def first_copy(o):
        peer = (t + o) % n_term
        return pltpu.make_async_remote_copy(
            part_ref.at[pl.ds(pl.multiple_of(peer * rows_out, 8), rows_out), :], first_ref.at[t],
            first_send.at[o - 1], first_recv.at[o - 1],
            device_id={"term": peer}, device_id_type=MESH,
        )

    def last_copy(o):
        peer = (t + o) % n_term
        return pltpu.make_async_remote_copy(
            code_ref.at[pl.ds(pl.multiple_of(peer * rows_out, 16), rows_out), :], last_ref.at[t],
            last_send.at[o - 1], last_recv.at[o - 1],
            device_id={"term": peer}, device_id_type=MESH,
        )

    def top_copy(o):
        return pltpu.make_async_remote_copy(
            top_ref.at[t], top_ref.at[t], top_send.at[o - 1], top_recv.at[o - 1],
            device_id={"term": (t + o) % n_term}, device_id_type=MESH,
        )

    def ws_copy(o):
        return pltpu.make_async_remote_copy(
            ws_ref.at[d], ws_ref.at[d], ws_send.at[o - 1], ws_recv.at[o - 1],
            device_id={"doc": (d + o) % n_doc}, device_id_type=MESH,
        )

    for o in range(1, n_term):
        fb_copy(o).start()
    for o in range(1, n_term):
        first_copy(o).start()
    own_rows = pl.ds(pl.multiple_of(t * rows_out, 8), rows_out)
    first_ref[t] = part_ref[own_rows, :]
    for o in range(1, n_term):
        fb_copy(o).wait_recv()
    fb_sum = fb_ref[0]
    for s in range(1, n_term):
        fb_sum = fb_sum + fb_ref[s]
    fb_row = jnp.sum(fb_sum, axis=0, keepdims=True)
    mix_ref[...] = (sel_ref[...] * fb_row).astype(bf16)

    ones = jnp.ones((16, docs), bf16)
    ws_ref[d] = dot_nt(ones, mix_ref[...])[:8]
    for o in range(1, n_doc):
        ws_copy(o).start()

    def copy_of(step, c, src, dst, peer):
        return pltpu.make_async_remote_copy(
            src, dst, pipe_send.at[step, c], pipe_recv.at[step, c],
            device_id={"doc": peer}, device_id_type=MESH,
        )

    twin = d + 1 - 2 * core

    def way(c):
        odd = c % 2
        even = 1 - odd
        in1 = even * bit1 + odd * bit2
        in2 = even * bit2 + odd * bit1
        peer1 = d + (even * 2 + odd * 4) * (1 - 2 * in1)
        peer2 = d + (even * 4 + odd * 2) * (1 - 2 * in2)
        return in1, in2, peer1, peer2

    def rows(start, size):
        return pl.ds(pl.multiple_of(start, 16), size)

    def exchange(step, c):
        in1, in2, peer1, peer2 = way(c)
        here = cols(c)
        if step == 0:
            return copy_of(0, c, nb_ref.at[rows((1 - core) * half, half), here], tw_ref.at[:, here], twin)
        if step == 1:
            return copy_of(1, c, s1_ref.at[rows((1 - in1) * quarter, quarter), here], a_ref.at[:, here], peer1)
        if step == 2:
            return copy_of(2, c, s2_ref.at[rows((1 - in2) * eighth, eighth), here], b_ref.at[:, here], peer2)
        base = core * half
        if step == 3:
            at = e_ref.at[rows(base + in1 * quarter + in2 * eighth, eighth), here]
            return copy_of(3, c, at, at, peer2)
        if step == 4:
            at = e_ref.at[rows(base + in1 * quarter, quarter), here]
            return copy_of(4, c, at, at, peer1)
        at = e_ref.at[rows(base, half), here]
        return copy_of(5, c, at, at, twin)

    acc_ref[...] = jnp.zeros_like(acc_ref)
    eye = (
        lax.broadcasted_iota(jnp.int32, (queries, queries), 0)
        == lax.broadcasted_iota(jnp.int32, (queries, queries), 1)
    )

    def step1(c):
        exchange(0, c).wait_recv()
        here = cols(c)
        s1_ref[:, here] = (
            nb_ref[rows(core * half, half), here].astype(f32) + tw_ref[:, here].astype(f32)
        ).astype(bf16)
        exchange(1, c).start()

    def step2(c):
        in1, in2, _, _ = way(c)
        exchange(1, c).wait_recv()
        here = cols(c)
        s2_ref[:, here] = (
            s1_ref[rows(in1 * quarter, quarter), here].astype(f32) + a_ref[:, here].astype(f32)
        ).astype(bf16)
        exchange(2, c).start()

    def step3(c):
        in1, in2, _, _ = way(c)
        exchange(2, c).wait_recv()
        here = cols(c)
        numerator = s2_ref[rows(in2 * eighth, eighth), here].astype(f32) + b_ref[:, here].astype(f32)
        mine = rows(core * half + in1 * quarter + in2 * eighth, eighth)
        total = wcol_ref[mine, :][:, 0:1]
        e_ref[mine, here] = (q_ref[mine, here] + expansion_weight * numerator / total).astype(bf16)
        exchange(3, c).start()

    def step4(c):
        exchange(3, c).wait_recv()
        exchange(4, c).start()

    def step5(c):
        exchange(4, c).wait_recv()
        exchange(5, c).start()

    def step0(c):
        here = cols(c)
        nb_ref[:, here] = jnp.dot(mix_ref[...], p_ref[:, here], preferred_element_type=f32).astype(bf16)
        exchange(0, c).start()

    def step6(c):
        exchange(5, c).wait_recv()
        here = cols(c)
        acc_ref[...] += dot_nt(e_ref[:, here], p_ref[:, here])

    def weights():
        for o in range(1, n_doc):
            ws_copy(o).wait_recv()
        total = ws_ref[0]
        for o in range(1, n_doc):
            total = total + ws_ref[o]
        column = jnp.sum(jnp.where(eye, total[0:1, :], 0.0), axis=1, keepdims=True)
        wcol_ref[...] = jnp.broadcast_to(column, wcol_ref.shape)

    body = (step0, step1, step2, step3, step4, step5, step6)
    for k, c in plan(chunks, queries * width * 2e-6):
        if (k, c) == (3, 0):
            weights()
        body[k](c)

    top = jnp.maximum(jnp.max(acc_ref[...], axis=1, keepdims=True), 1e-30)
    code_ref[...] = jnp.round(acc_ref[...] * (32767.0 / top)).astype(jnp.int32).astype(jnp.int16)
    for o in range(1, n_term):
        last_copy(o).start()
    top_ref[t] = jnp.broadcast_to(
        jnp.sum(jnp.where(eye, top, 0.0), axis=0, keepdims=True) / 32767.0, (8, queries)
    )
    for o in range(1, n_term):
        top_copy(o).start()

    for o in range(1, n_term):
        first_copy(o).wait_recv()
    total = first_ref[0]
    for s in range(1, n_term):
        total = total + first_ref[s]
    first_out[...] = total

    for o in range(1, n_term):
        top_copy(o).wait_recv()
    for s in range(n_term):
        column = jnp.sum(jnp.where(eye, top_ref[s][0:1, :], 0.0), axis=1, keepdims=True)
        wcol_ref[...] = jnp.broadcast_to(column, wcol_ref.shape)
        tops_ref[s] = wcol_ref[own_rows, :]
    total = acc_ref[own_rows, :]
    for o in range(1, n_term):
        last_copy(o).wait_recv()
        s = (t + n_term - o) % n_term
        steps = last_ref[s].astype(jnp.int32).astype(f32)
        total = total + steps * tops_ref[s][:, 0:1]
    final_out[...] = total

    for o in range(1, n_term):
        fb_copy(o).wait_send()
        first_copy(o).wait_send()
        last_copy(o).wait_send()
        top_copy(o).wait_send()
    for o in range(1, n_doc):
        ws_copy(o).wait_send()

    def drain(c, carry):
        for step in range(6):
            exchange(step, c).wait_send()
        return carry

    lax.fori_loop(0, chunks, drain, 0)


def fused(postings, query_terms, query_levels, feedback_ids):
    docs, width = postings.shape
    queries, slots = query_terms.shape
    n_term, n_doc = lax.axis_size("term"), lax.axis_size("doc")
    chunks = next(c for c in (10, 6, 4, 2, 1) if width % (c * LANES) == 0)
    loads = next(c for c in (5, 3, 2, 1) if width % (c * LANES) == 0)
    rows_out = queries // n_term
    group = 8 * slots
    vmem = pltpu.VMEM
    dma = pltpu.SemaphoreType.DMA
    out = jax.ShapeDtypeStruct((rows_out, docs), f32)
    return pl.pallas_call(
        functools.partial(fused_kernel, n_term, n_doc, chunks, loads),
        out_shape=(out, out),
        in_specs=[pl.BlockSpec(memory_space=pl.ANY)] + [pl.BlockSpec(memory_space=pltpu.VMEM)] * 3,
        out_specs=(pl.BlockSpec(memory_space=pltpu.VMEM),) * 2,
        scratch_shapes=[
            vmem((docs, width), bf16),
            vmem((queries, width), f32),
            vmem((queries // 8, group), f32),
            vmem((queries // 8, group), f32),
            vmem((queries // 8, group), f32),
            vmem((queries, docs), f32),
            vmem((queries, docs), f32),
            vmem((queries, docs), bf16),
            vmem((n_term, 8, docs), f32),
            vmem((n_term, rows_out, docs), f32),
            vmem((n_doc, 8, queries), f32),
            vmem((queries, LANES), f32),
            vmem((queries, width), bf16),
            vmem((queries // 2, width), bf16),
            vmem((queries // 2, width), bf16),
            vmem((queries // 4, width), bf16),
            vmem((queries // 4, width), bf16),
            vmem((queries // 8, width), bf16),
            vmem((queries, width), bf16),
            vmem((queries, docs), f32),
            vmem((queries, docs), jnp.int16),
            vmem((n_term, rows_out, docs), jnp.int16),
            vmem((n_term, 8, queries), f32),
            vmem((n_term, rows_out, LANES), f32),
            dma((loads,)),
            dma((n_term - 1,)),
            dma((n_term - 1,)),
            dma((n_term - 1,)),
            dma((n_term - 1,)),
            dma((n_doc - 1,)),
            dma((n_doc - 1,)),
            dma((6, chunks)),
            dma((6, chunks)),
            dma((n_term - 1,)),
            dma((n_term - 1,)),
            dma((n_term - 1,)),
            dma((n_term - 1,)),
        ],
        compiler_params=pltpu.CompilerParams(
            collective_id=0, has_side_effects=True, vmem_limit_bytes=48 * 1024 * 1024
        ),
        cost_estimate=pl.CostEstimate(
            flops=6 * queries * docs * width, bytes_accessed=2 * docs * width, transcendentals=0
        ),
        name="fused_feedback",
    )(postings, query_terms.T, query_levels.T, feedback_ids.T)


def query_slice(query_terms, query_levels, width, offset):
    columns = offset + lax.iota(jnp.int32, width)

    def add_term(position, total):
        ids_now = lax.dynamic_index_in_dim(query_terms, position, 1, keepdims=True)
        weight_now = (
            lax.dynamic_index_in_dim(query_levels, position, 1, keepdims=True).astype(f32) / 100.0
        )
        return total + jnp.where(ids_now == columns[None, :], weight_now, 0.0)

    initial = jnp.zeros((query_terms.shape[0], width), f32)
    return lax.fori_loop(0, query_terms.shape[1], add_term, initial)


def general(postings, query_terms, query_levels, feedback_ids):
    doc_rows, width = postings.shape
    queries = query_terms.shape[0]
    group_rows = queries // lax.axis_size("term")
    term_index = lax.axis_index("term")
    doc_index = lax.axis_index("doc")
    query_part = query_slice(query_terms, query_levels, width, term_index * width)
    local_slot = feedback_ids - doc_index * doc_rows
    positions = lax.iota(jnp.int32, doc_rows)
    selector = (local_slot[:, :, None] == positions[None, None, :]).astype(f32)
    first_all = lax.psum(dot_nt(query_part.astype(bf16), postings), "term")
    first_scores = lax.dynamic_slice_in_dim(first_all, term_index * group_rows, group_rows, 0)
    feedback = jnp.sum(selector * first_all[:, None, :], axis=2).astype(bf16).astype(f32)
    mixing = jnp.sum(selector * feedback[:, :, None], axis=1).astype(bf16)
    numerator = jnp.dot(mixing, postings, preferred_element_type=f32)
    numerator, weight_sum = lax.psum((numerator, jnp.sum(feedback, axis=1)), "doc")
    expanded = (query_part + expansion_weight * numerator / weight_sum[:, None]).astype(bf16)
    final_scores = lax.psum_scatter(
        dot_nt(expanded, postings), "term", scatter_dimension=0, tiled=True
    )
    return first_scores, final_scores


def per_device(postings, query_terms, query_levels, feedback_ids):
    docs, width = postings.shape
    queries, slots = query_terms.shape
    fits = (
        lax.axis_size("doc") == 8
        and lax.axis_size("term") > 1
        and queries == LANES
        and queries % (16 * lax.axis_size("term")) == 0
        and width % LANES == 0
        and docs % LANES == 0
    )
    run = fused if fits else general
    return run(postings, query_terms, query_levels, feedback_ids)


def solution(mesh):
    return jax.shard_map(
        per_device,
        mesh=mesh,
        in_specs=(P("doc", "term"), P(), P(), P()),
        out_specs=(P("term", "doc"), P("term", "doc")),
        check_vma=False,
    )
```

```python
import functools

import jax
import jax.numpy as jnp
from jax import lax
from jax.experimental import pallas as pl
from jax.experimental.pallas import tpu as pltpu
from jax.sharding import PartitionSpec as P

expansion_weight = 0.25
MESH = pl.DeviceIdType.MESH
LANES = 128
NT = (((1,), (1,)), ((), ()))
f32 = jnp.float32
bf16 = jnp.bfloat16


def dot_nt(a, b):
    return lax.dot_general(a, b, NT, preferred_element_type=f32)


def plan(chunks, mega):
    part = mega / chunks
    send = (part * 0.83, part * 5.0, part * 2.5, part * 2.5, part * 5.0, part * 0.83)
    work = (3.0 / chunks, 1.0 / chunks, 0.5 / chunks, 1.0 / chunks, 0.02, 0.02, 4.0 / chunks)
    free = {"twin": 0.0, "x": 0.0, "y": 0.0}
    arrival, at, order = {}, [0] * 7, []
    now = 0.0
    rank = (5, 4, 3, 2, 1, 0, 6)

    def due(k):
        return 0.0 if k == 0 else arrival.get((k - 1, at[k]), float("inf"))

    while at[6] < chunks:
        open_steps = [k for k in rank if at[k] < chunks]
        ready = [k for k in open_steps if due(k) <= now]
        k = ready[0] if ready else min(open_steps, key=due)
        c = at[k]
        now = max(now, due(k)) + work[k]
        if k < 6:
            link = "twin" if k in (0, 5) else "xy"[(c + (k in (2, 3))) % 2]
            free[link] = max(now, free[link]) + send[k]
            arrival[k, c] = free[link] + 1.0
        at[k] += 1
        order.append((k, c))
    return order


def fused_kernel(
    n_term, n_doc, chunks, loads,
    postings, terms, levels, ids, first_out, final_out,
    p_ref, q_ref, hi_ref, lo_ref, lev_ref, part_ref, tall_ref, sel_ref, mix_ref,
    fb_ref, first_ref, ws_ref, wcol_ref, nb_ref, tw_ref, s1_ref, a_ref, s2_ref, b_ref,
    e_ref, acc_ref, code_ref, last_ref, top_ref, tops_ref,
    p_sem, fb_send, fb_recv, first_send, first_recv, ws_send, ws_recv,
    pipe_send, pipe_recv, last_send, last_recv, top_send, top_recv,
):
    t = lax.axis_index("term")
    d = lax.axis_index("doc")
    docs, width = p_ref.shape
    slots, queries = terms.shape
    cw = width // chunks
    lw = width // loads
    his = width // LANES
    rows_out = queries // n_term
    half, quarter, eighth = queries // 2, queries // 4, queries // 8

    core = d % 2
    bit1 = (d // 2) % 2
    bit2 = (d // 4) % 2

    def cols(c):
        return pl.ds(pl.multiple_of(c * cw, LANES), cw)

    def load_cols(c):
        return pl.ds(pl.multiple_of(c * lw, LANES), lw)

    def load(c):
        here = load_cols(c)
        return pltpu.make_async_copy(postings.at[:, here], p_ref.at[:, here], p_sem.at[c])

    for c in range(loads):
        load(c).start()

    barrier = pltpu.get_barrier_semaphore()
    for o in range(1, n_term):
        pl.semaphore_signal(barrier, inc=1, device_id={"term": (t + o) % n_term}, device_id_type=MESH)
    for o in range(1, n_doc):
        pl.semaphore_signal(barrier, inc=1, device_id={"doc": (d + o) % n_doc}, device_id_type=MESH)

    group = 8 * slots
    spread = (
        lax.broadcasted_iota(jnp.int32, (slots, group), 0)
        == lax.broadcasted_iota(jnp.int32, (slots, group), 1) % slots
    ).astype(bf16)
    own = (
        lax.broadcasted_iota(jnp.int32, (queries, group), 0) % 8
        == lax.broadcasted_iota(jnp.int32, (queries, group), 1) // slots
    )

    def lay(values):
        wide = lax.dot_general(
            values.astype(f32).astype(bf16), spread, (((0,), (0,)), ((), ())), preferred_element_type=f32
        )
        return jnp.sum(jnp.where(own, wide, 0.0).reshape(queries // 8, 8, group), axis=1)

    ids_now = terms[...]
    q8 = (lax.broadcasted_iota(jnp.int32, (queries // 8, group), 1) // slots).astype(f32)
    hi = lay(ids_now // LANES) - (t * his).astype(f32)
    hi_ref[...] = hi * 8.0 + q8
    lo_ref[...] = lay(ids_now % LANES)
    lev_ref[...] = lay(levels[...])

    row_code = lax.broadcasted_iota(jnp.int32, (his * 8, group), 0).astype(f32)
    lane_code = lax.broadcasted_iota(jnp.int32, (LANES, group), 0).astype(f32)

    def build_one(g):
        left = jnp.where(
            hi_ref[pl.ds(g, 1), :] == row_code, lev_ref[pl.ds(g, 1), :], 0.0
        ).astype(bf16)
        right = jnp.where(lo_ref[pl.ds(g, 1), :] == lane_code, 1.0, 0.0).astype(bf16)
        block = dot_nt(left, right) * 0.01
        rows = pl.ds(pl.multiple_of(g * 8, 8), 8)
        for h in range(his):
            q_ref[rows, h * LANES : (h + 1) * LANES] = block[h * 8 : (h + 1) * 8]

    def build(g, carry):
        for i in range(4):
            build_one(g * 4 + i)
        return carry

    lax.fori_loop(0, queries // 32, build, 0)

    place = lax.broadcasted_iota(jnp.int32, (queries, docs), 1)
    local = ids[...].T - d * docs
    sel = place == local[:, 0:1]
    for j in range(1, local.shape[1]):
        sel = sel | (place == local[:, j : j + 1])
    sel_ref[...] = jnp.where(sel, 1.0, 0.0)

    tall_ref[...] = jnp.zeros_like(tall_ref)

    def score(c, carry):
        load(c).wait()
        tall_ref[...] += dot_nt(p_ref[:, load_cols(c)], q_ref[:, load_cols(c)].astype(bf16))
        return carry

    lax.fori_loop(0, loads, score, 0)
    part_ref[...] = tall_ref[...].T

    pl.semaphore_wait(barrier, n_term + n_doc - 2)

    fb_ref[t] = jnp.sum((sel_ref[...] * part_ref[...]).reshape(queries // 8, 8, docs), axis=0)

    def fb_copy(o):
        return pltpu.make_async_remote_copy(
            fb_ref.at[t], fb_ref.at[t], fb_send.at[o - 1], fb_recv.at[o - 1],
            device_id={"term": (t + o) % n_term}, device_id_type=MESH,
        )

    def first_copy(o):
        peer = (t + o) % n_term
        return pltpu.make_async_remote_copy(
            part_ref.at[pl.ds(pl.multiple_of(peer * rows_out, 8), rows_out), :], first_ref.at[t],
            first_send.at[o - 1], first_recv.at[o - 1],
            device_id={"term": peer}, device_id_type=MESH,
        )

    def last_copy(o):
        peer = (t + o) % n_term
        return pltpu.make_async_remote_copy(
            code_ref.at[pl.ds(pl.multiple_of(peer * rows_out, 16), rows_out), :], last_ref.at[t],
            last_send.at[o - 1], last_recv.at[o - 1],
            device_id={"term": peer}, device_id_type=MESH,
        )

    def top_copy(o):
        return pltpu.make_async_remote_copy(
            top_ref.at[t], top_ref.at[t], top_send.at[o - 1], top_recv.at[o - 1],
            device_id={"term": (t + o) % n_term}, device_id_type=MESH,
        )

    def ws_copy(o):
        return pltpu.make_async_remote_copy(
            ws_ref.at[d], ws_ref.at[d], ws_send.at[o - 1], ws_recv.at[o - 1],
            device_id={"doc": (d + o) % n_doc}, device_id_type=MESH,
        )

    for o in range(1, n_term):
        fb_copy(o).start()
    for o in range(1, n_term):
        first_copy(o).start()
    own_rows = pl.ds(pl.multiple_of(t * rows_out, 8), rows_out)
    first_ref[t] = part_ref[own_rows, :]
    for o in range(1, n_term):
        fb_copy(o).wait_recv()
    fb_sum = fb_ref[0]
    for s in range(1, n_term):
        fb_sum = fb_sum + fb_ref[s]
    fb_row = jnp.sum(fb_sum, axis=0, keepdims=True)
    mix_ref[...] = (sel_ref[...] * fb_row).astype(bf16)

    ones = jnp.ones((16, docs), bf16)
    ws_ref[d] = dot_nt(ones, mix_ref[...])[:8]
    for o in range(1, n_doc):
        ws_copy(o).start()

    def copy_of(step, c, src, dst, peer):
        return pltpu.make_async_remote_copy(
            src, dst, pipe_send.at[step, c], pipe_recv.at[step, c],
            device_id={"doc": peer}, device_id_type=MESH,
        )

    twin = d + 1 - 2 * core

    def way(c):
        odd = c % 2
        even = 1 - odd
        in1 = even * bit1 + odd * bit2
        in2 = even * bit2 + odd * bit1
        peer1 = d + (even * 2 + odd * 4) * (1 - 2 * in1)
        peer2 = d + (even * 4 + odd * 2) * (1 - 2 * in2)
        return in1, in2, peer1, peer2

    def rows(start, size):
        return pl.ds(pl.multiple_of(start, 16), size)

    def exchange(step, c):
        in1, in2, peer1, peer2 = way(c)
        here = cols(c)
        if step == 0:
            return copy_of(0, c, nb_ref.at[rows((1 - core) * half, half), here], tw_ref.at[:, here], twin)
        if step == 1:
            return copy_of(1, c, s1_ref.at[rows((1 - in1) * quarter, quarter), here], a_ref.at[:, here], peer1)
        if step == 2:
            return copy_of(2, c, s2_ref.at[rows((1 - in2) * eighth, eighth), here], b_ref.at[:, here], peer2)
        base = core * half
        if step == 3:
            at = e_ref.at[rows(base + in1 * quarter + in2 * eighth, eighth), here]
            return copy_of(3, c, at, at, peer2)
        if step == 4:
            at = e_ref.at[rows(base + in1 * quarter, quarter), here]
            return copy_of(4, c, at, at, peer1)
        at = e_ref.at[rows(base, half), here]
        return copy_of(5, c, at, at, twin)

    tall_ref[...] = jnp.zeros_like(tall_ref)
    eye = (
        lax.broadcasted_iota(jnp.int32, (queries, queries), 0)
        == lax.broadcasted_iota(jnp.int32, (queries, queries), 1)
    )

    def step1(c):
        exchange(0, c).wait_recv()
        here = cols(c)
        s1_ref[:, here] = (
            nb_ref[rows(core * half, half), here].astype(f32) + tw_ref[:, here].astype(f32)
        ).astype(bf16)
        exchange(1, c).start()

    def step2(c):
        in1, in2, _, _ = way(c)
        exchange(1, c).wait_recv()
        here = cols(c)
        s2_ref[:, here] = (
            s1_ref[rows(in1 * quarter, quarter), here].astype(f32) + a_ref[:, here].astype(f32)
        ).astype(bf16)
        exchange(2, c).start()

    def step3(c):
        in1, in2, _, _ = way(c)
        exchange(2, c).wait_recv()
        here = cols(c)
        numerator = s2_ref[rows(in2 * eighth, eighth), here].astype(f32) + b_ref[:, here].astype(f32)
        mine = rows(core * half + in1 * quarter + in2 * eighth, eighth)
        total = wcol_ref[mine, :][:, 0:1]
        e_ref[mine, here] = (q_ref[mine, here] + expansion_weight * numerator / total).astype(bf16)
        exchange(3, c).start()

    def step4(c):
        exchange(3, c).wait_recv()
        exchange(4, c).start()

    def step5(c):
        exchange(4, c).wait_recv()
        exchange(5, c).start()

    def step0(c):
        here = cols(c)
        nb_ref[:, here] = jnp.dot(mix_ref[...], p_ref[:, here], preferred_element_type=f32).astype(bf16)
        exchange(0, c).start()

    def step6(c):
        exchange(5, c).wait_recv()
        here = cols(c)
        tall_ref[...] += dot_nt(p_ref[:, here], e_ref[:, here])

    def weights():
        for o in range(1, n_doc):
            ws_copy(o).wait_recv()
        total = ws_ref[0]
        for o in range(1, n_doc):
            total = total + ws_ref[o]
        column = jnp.sum(jnp.where(eye, total[0:1, :], 0.0), axis=1, keepdims=True)
        wcol_ref[...] = jnp.broadcast_to(column, wcol_ref.shape)

    body = (step0, step1, step2, step3, step4, step5, step6)
    for k, c in plan(chunks, queries * width * 2e-6):
        if (k, c) == (3, 0):
            weights()
        body[k](c)

    acc_ref[...] = tall_ref[...].T
    top = jnp.maximum(jnp.max(acc_ref[...], axis=1, keepdims=True), 1e-30)
    code_ref[...] = jnp.round(acc_ref[...] * (32767.0 / top)).astype(jnp.int32).astype(jnp.int16)
    for o in range(1, n_term):
        last_copy(o).start()
    top_ref[t] = jnp.broadcast_to(
        jnp.sum(jnp.where(eye, top, 0.0), axis=0, keepdims=True) / 32767.0, (8, queries)
    )
    for o in range(1, n_term):
        top_copy(o).start()

    for o in range(1, n_term):
        first_copy(o).wait_recv()
    total = first_ref[0]
    for s in range(1, n_term):
        total = total + first_ref[s]
    first_out[...] = total

    for o in range(1, n_term):
        top_copy(o).wait_recv()
    for s in range(n_term):
        column = jnp.sum(jnp.where(eye, top_ref[s][0:1, :], 0.0), axis=1, keepdims=True)
        wcol_ref[...] = jnp.broadcast_to(column, wcol_ref.shape)
        tops_ref[s] = wcol_ref[own_rows, :]
    total = acc_ref[own_rows, :]
    for o in range(1, n_term):
        last_copy(o).wait_recv()
        s = (t + n_term - o) % n_term
        steps = last_ref[s].astype(jnp.int32).astype(f32)
        total = total + steps * tops_ref[s][:, 0:1]
    final_out[...] = total

    for o in range(1, n_term):
        fb_copy(o).wait_send()
        first_copy(o).wait_send()
        last_copy(o).wait_send()
        top_copy(o).wait_send()
    for o in range(1, n_doc):
        ws_copy(o).wait_send()

    def drain(c, carry):
        for step in range(6):
            exchange(step, c).wait_send()
        return carry

    lax.fori_loop(0, chunks, drain, 0)


def fused(postings, query_terms, query_levels, feedback_ids):
    docs, width = postings.shape
    queries, slots = query_terms.shape
    n_term, n_doc = lax.axis_size("term"), lax.axis_size("doc")
    chunks = next(c for c in (10, 6, 4, 2, 1) if width % (c * LANES) == 0)
    loads = next(c for c in (5, 3, 2, 1) if width % (c * LANES) == 0)
    rows_out = queries // n_term
    group = 8 * slots
    vmem = pltpu.VMEM
    dma = pltpu.SemaphoreType.DMA
    out = jax.ShapeDtypeStruct((rows_out, docs), f32)
    return pl.pallas_call(
        functools.partial(fused_kernel, n_term, n_doc, chunks, loads),
        out_shape=(out, out),
        in_specs=[pl.BlockSpec(memory_space=pl.ANY)] + [pl.BlockSpec(memory_space=pltpu.VMEM)] * 3,
        out_specs=(pl.BlockSpec(memory_space=pltpu.VMEM),) * 2,
        scratch_shapes=[
            vmem((docs, width), bf16),
            vmem((queries, width), f32),
            vmem((queries // 8, group), f32),
            vmem((queries // 8, group), f32),
            vmem((queries // 8, group), f32),
            vmem((queries, docs), f32),
            vmem((docs, queries), f32),
            vmem((queries, docs), f32),
            vmem((queries, docs), bf16),
            vmem((n_term, 8, docs), f32),
            vmem((n_term, rows_out, docs), f32),
            vmem((n_doc, 8, queries), f32),
            vmem((queries, LANES), f32),
            vmem((queries, width), bf16),
            vmem((queries // 2, width), bf16),
            vmem((queries // 2, width), bf16),
            vmem((queries // 4, width), bf16),
            vmem((queries // 4, width), bf16),
            vmem((queries // 8, width), bf16),
            vmem((queries, width), bf16),
            vmem((queries, docs), f32),
            vmem((queries, docs), jnp.int16),
            vmem((n_term, rows_out, docs), jnp.int16),
            vmem((n_term, 8, queries), f32),
            vmem((n_term, rows_out, LANES), f32),
            dma((loads,)),
            dma((n_term - 1,)),
            dma((n_term - 1,)),
            dma((n_term - 1,)),
            dma((n_term - 1,)),
            dma((n_doc - 1,)),
            dma((n_doc - 1,)),
            dma((6, chunks)),
            dma((6, chunks)),
            dma((n_term - 1,)),
            dma((n_term - 1,)),
            dma((n_term - 1,)),
            dma((n_term - 1,)),
        ],
        compiler_params=pltpu.CompilerParams(
            collective_id=0, has_side_effects=True, vmem_limit_bytes=48 * 1024 * 1024
        ),
        cost_estimate=pl.CostEstimate(
            flops=6 * queries * docs * width, bytes_accessed=2 * docs * width, transcendentals=0
        ),
        name="fused_feedback",
    )(postings, query_terms.T, query_levels.T, feedback_ids.T)


def query_slice(query_terms, query_levels, width, offset):
    columns = offset + lax.iota(jnp.int32, width)

    def add_term(position, total):
        ids_now = lax.dynamic_index_in_dim(query_terms, position, 1, keepdims=True)
        weight_now = (
            lax.dynamic_index_in_dim(query_levels, position, 1, keepdims=True).astype(f32) / 100.0
        )
        return total + jnp.where(ids_now == columns[None, :], weight_now, 0.0)

    initial = jnp.zeros((query_terms.shape[0], width), f32)
    return lax.fori_loop(0, query_terms.shape[1], add_term, initial)


def general(postings, query_terms, query_levels, feedback_ids):
    doc_rows, width = postings.shape
    queries = query_terms.shape[0]
    group_rows = queries // lax.axis_size("term")
    term_index = lax.axis_index("term")
    doc_index = lax.axis_index("doc")
    query_part = query_slice(query_terms, query_levels, width, term_index * width)
    local_slot = feedback_ids - doc_index * doc_rows
    positions = lax.iota(jnp.int32, doc_rows)
    selector = (local_slot[:, :, None] == positions[None, None, :]).astype(f32)
    first_all = lax.psum(dot_nt(query_part.astype(bf16), postings), "term")
    first_scores = lax.dynamic_slice_in_dim(first_all, term_index * group_rows, group_rows, 0)
    feedback = jnp.sum(selector * first_all[:, None, :], axis=2).astype(bf16).astype(f32)
    mixing = jnp.sum(selector * feedback[:, :, None], axis=1).astype(bf16)
    numerator = jnp.dot(mixing, postings, preferred_element_type=f32)
    numerator, weight_sum = lax.psum((numerator, jnp.sum(feedback, axis=1)), "doc")
    expanded = (query_part + expansion_weight * numerator / weight_sum[:, None]).astype(bf16)
    final_scores = lax.psum_scatter(
        dot_nt(expanded, postings), "term", scatter_dimension=0, tiled=True
    )
    return first_scores, final_scores


def per_device(postings, query_terms, query_levels, feedback_ids):
    docs, width = postings.shape
    queries, slots = query_terms.shape
    fits = (
        lax.axis_size("doc") == 8
        and lax.axis_size("term") > 1
        and queries == LANES
        and queries % (16 * lax.axis_size("term")) == 0
        and width % LANES == 0
        and docs % LANES == 0
    )
    run = fused if fits else general
    return run(postings, query_terms, query_levels, feedback_ids)


def solution(mesh):
    return jax.shard_map(
        per_device,
        mesh=mesh,
        in_specs=(P("doc", "term"), P(), P(), P()),
        out_specs=(P("term", "doc"), P("term", "doc")),
        check_vma=False,
    )
```

```python
import functools

import jax
import jax.numpy as jnp
from jax import lax
from jax.experimental import pallas as pl
from jax.experimental.pallas import tpu as pltpu
from jax.sharding import PartitionSpec as P

expansion_weight = 0.25
MESH = pl.DeviceIdType.MESH
LANES = 128
BIN = 256
NT = (((1,), (1,)), ((), ()))
f32 = jnp.float32
bf16 = jnp.bfloat16


def dot_nt(a, b):
    return lax.dot_general(a, b, NT, preferred_element_type=f32)


def plan(chunks, mega):
    part = mega / chunks
    send = (part * 0.83, part * 5.0, part * 2.5, part * 2.5, part * 5.0, part * 0.83)
    work = (3.0 / chunks, 1.0 / chunks, 0.5 / chunks, 1.0 / chunks, 0.02, 0.02, 4.0 / chunks)
    free = {"twin": 0.0, "x": 0.0, "y": 0.0}
    arrival, at, order = {}, [0] * 7, []
    now = 0.0
    rank = (5, 4, 3, 2, 1, 0, 6)

    def due(k):
        return 0.0 if k == 0 else arrival.get((k - 1, at[k]), float("inf"))

    while at[6] < chunks:
        open_steps = [k for k in rank if at[k] < chunks]
        ready = [k for k in open_steps if due(k) <= now]
        k = ready[0] if ready else min(open_steps, key=due)
        c = at[k]
        now = max(now, due(k)) + work[k]
        if k < 6:
            link = "twin" if k in (0, 5) else "xy"[(c + (k in (2, 3))) % 2]
            free[link] = max(now, free[link]) + send[k]
            arrival[k, c] = free[link] + 1.0
        at[k] += 1
        order.append((k, c))
    return order


def fused_kernel(
    n_term, n_doc, chunks, loads,
    slots, postings, small, first_out, final_out,
    p_ref, q_ref, hi_ref, lo_ref, lev_ref, part_ref, sel_ref, mix_ref,
    fb_ref, first_ref, ws_ref, wcol_ref, nb_ref, tw_ref, s1_ref, a_ref, s2_ref, b_ref,
    e_ref, acc_ref, code_ref, last_ref, top_ref, tops_ref,
    p_sem, fb_send, fb_recv, first_send, first_recv, ws_send, ws_recv,
    pipe_send, pipe_recv, last_send, last_recv, top_send, top_recv,
):
    t = lax.axis_index("term")
    d = lax.axis_index("doc")
    docs, width = p_ref.shape
    queries = small.shape[1]
    cw = width // chunks
    lw = width // loads
    his = width // BIN
    rows_out = queries // n_term
    half, quarter, eighth = queries // 2, queries // 4, queries // 8

    core = d % 2
    bit1 = (d // 2) % 2
    bit2 = (d // 4) % 2

    def cols(c):
        return pl.ds(pl.multiple_of(c * cw, LANES), cw)

    def load_cols(c):
        return pl.ds(pl.multiple_of(c * lw, LANES), lw)

    def load(c):
        here = load_cols(c)
        return pltpu.make_async_copy(postings.at[:, here], p_ref.at[:, here], p_sem.at[c])

    for c in range(loads):
        load(c).start()

    barrier = pltpu.get_barrier_semaphore()
    for o in range(1, n_term):
        pl.semaphore_signal(barrier, inc=1, device_id={"term": (t + o) % n_term}, device_id_type=MESH)
    for o in range(1, n_doc):
        pl.semaphore_signal(barrier, inc=1, device_id={"doc": (d + o) % n_doc}, device_id_type=MESH)

    group = 8 * slots
    spread = (
        lax.broadcasted_iota(jnp.int32, (slots, group), 0)
        == lax.broadcasted_iota(jnp.int32, (slots, group), 1) % slots
    ).astype(bf16)
    own = (
        lax.broadcasted_iota(jnp.int32, (queries, group), 0) % 8
        == lax.broadcasted_iota(jnp.int32, (queries, group), 1) // slots
    )

    def lay(values):
        wide = lax.dot_general(
            values.astype(f32).astype(bf16), spread, (((0,), (0,)), ((), ())), preferred_element_type=f32
        )
        return jnp.sum(jnp.where(own, wide, 0.0).reshape(queries // 8, 8, group), axis=1)

    ids_now = small[:slots]
    q8 = (lax.broadcasted_iota(jnp.int32, (queries // 8, group), 1) // slots).astype(f32)
    hi = lay(ids_now // BIN) - (t * his).astype(f32)
    hi_ref[...] = hi * 8.0 + q8
    lo_ref[...] = lay(ids_now % BIN)
    lev_ref[...] = lay(small[slots : 2 * slots])

    row_code = lax.broadcasted_iota(jnp.int32, (his * 8, group), 0).astype(f32)
    lane_code = lax.broadcasted_iota(jnp.int32, (BIN, group), 0).astype(f32)

    def build_one(g):
        left = jnp.where(
            hi_ref[pl.ds(g, 1), :] == row_code, lev_ref[pl.ds(g, 1), :], 0.0
        ).astype(bf16)
        right = jnp.where(lo_ref[pl.ds(g, 1), :] == lane_code, 1.0, 0.0).astype(bf16)
        block = dot_nt(left, right) * 0.01
        rows = pl.ds(pl.multiple_of(g * 8, 8), 8)
        for h in range(his):
            q_ref[rows, h * BIN : (h + 1) * BIN] = block[h * 8 : (h + 1) * 8]

    def build(g, carry):
        for i in range(4):
            build_one(g * 4 + i)
        return carry

    lax.fori_loop(0, queries // 32, build, 0)

    place = lax.broadcasted_iota(jnp.int32, (queries, docs), 1)
    local = small[2 * slots :].T - d * docs
    sel = place == local[:, 0:1]
    for j in range(1, local.shape[1]):
        sel = sel | (place == local[:, j : j + 1])
    sel_ref[...] = jnp.where(sel, 1.0, 0.0)

    part_ref[...] = jnp.zeros_like(part_ref)

    def score(c, carry):
        load(c).wait()
        part_ref[...] += dot_nt(q_ref[:, load_cols(c)].astype(bf16), p_ref[:, load_cols(c)])
        return carry

    lax.fori_loop(0, loads, score, 0)

    pl.semaphore_wait(barrier, n_term + n_doc - 2)

    fb_ref[t] = jnp.sum((sel_ref[...] * part_ref[...]).reshape(queries // 8, 8, docs), axis=0)

    def fb_copy(o):
        return pltpu.make_async_remote_copy(
            fb_ref.at[t], fb_ref.at[t], fb_send.at[o - 1], fb_recv.at[o - 1],
            device_id={"term": (t + o) % n_term}, device_id_type=MESH,
        )

    def first_copy(o):
        peer = (t + o) % n_term
        return pltpu.make_async_remote_copy(
            part_ref.at[pl.ds(pl.multiple_of(peer * rows_out, 8), rows_out), :], first_ref.at[t],
            first_send.at[o - 1], first_recv.at[o - 1],
            device_id={"term": peer}, device_id_type=MESH,
        )

    def last_copy(o):
        peer = (t + o) % n_term
        return pltpu.make_async_remote_copy(
            code_ref.at[pl.ds(pl.multiple_of(peer * rows_out, 16), rows_out), :], last_ref.at[t],
            last_send.at[o - 1], last_recv.at[o - 1],
            device_id={"term": peer}, device_id_type=MESH,
        )

    def top_copy(o):
        return pltpu.make_async_remote_copy(
            top_ref.at[t], top_ref.at[t], top_send.at[o - 1], top_recv.at[o - 1],
            device_id={"term": (t + o) % n_term}, device_id_type=MESH,
        )

    def ws_copy(o):
        return pltpu.make_async_remote_copy(
            ws_ref.at[d], ws_ref.at[d], ws_send.at[o - 1], ws_recv.at[o - 1],
            device_id={"doc": (d + o) % n_doc}, device_id_type=MESH,
        )

    for o in range(1, n_term):
        fb_copy(o).start()
    for o in range(1, n_term):
        first_copy(o).start()
    own_rows = pl.ds(pl.multiple_of(t * rows_out, 8), rows_out)
    first_ref[t] = part_ref[own_rows, :]
    for o in range(1, n_term):
        fb_copy(o).wait_recv()
    fb_sum = fb_ref[0]
    for s in range(1, n_term):
        fb_sum = fb_sum + fb_ref[s]
    fb_row = jnp.sum(fb_sum, axis=0, keepdims=True)
    mix_ref[...] = (sel_ref[...] * fb_row).astype(bf16)

    ones = jnp.ones((16, docs), bf16)
    ws_ref[d] = dot_nt(ones, mix_ref[...])[:8]
    for o in range(1, n_doc):
        ws_copy(o).start()

    def copy_of(step, c, src, dst, peer):
        return pltpu.make_async_remote_copy(
            src, dst, pipe_send.at[step, c], pipe_recv.at[step, c],
            device_id={"doc": peer}, device_id_type=MESH,
        )

    twin = d + 1 - 2 * core

    def way(c):
        odd = c % 2
        even = 1 - odd
        in1 = even * bit1 + odd * bit2
        in2 = even * bit2 + odd * bit1
        peer1 = d + (even * 2 + odd * 4) * (1 - 2 * in1)
        peer2 = d + (even * 4 + odd * 2) * (1 - 2 * in2)
        return in1, in2, peer1, peer2

    def rows(start, size):
        return pl.ds(pl.multiple_of(start, 16), size)

    def exchange(step, c):
        in1, in2, peer1, peer2 = way(c)
        here = cols(c)
        if step == 0:
            return copy_of(0, c, nb_ref.at[rows((1 - core) * half, half), here], tw_ref.at[:, here], twin)
        if step == 1:
            return copy_of(1, c, s1_ref.at[rows((1 - in1) * quarter, quarter), here], a_ref.at[:, here], peer1)
        if step == 2:
            return copy_of(2, c, s2_ref.at[rows((1 - in2) * eighth, eighth), here], b_ref.at[:, here], peer2)
        base = core * half
        if step == 3:
            at = e_ref.at[rows(base + in1 * quarter + in2 * eighth, eighth), here]
            return copy_of(3, c, at, at, peer2)
        if step == 4:
            at = e_ref.at[rows(base + in1 * quarter, quarter), here]
            return copy_of(4, c, at, at, peer1)
        at = e_ref.at[rows(base, half), here]
        return copy_of(5, c, at, at, twin)

    acc_ref[...] = jnp.zeros_like(acc_ref)
    eye = (
        lax.broadcasted_iota(jnp.int32, (queries, queries), 0)
        == lax.broadcasted_iota(jnp.int32, (queries, queries), 1)
    )

    def step1(c):
        exchange(0, c).wait_recv()
        here = cols(c)
        s1_ref[:, here] = (
            nb_ref[rows(core * half, half), here].astype(f32) + tw_ref[:, here].astype(f32)
        ).astype(bf16)
        exchange(1, c).start()

    def step2(c):
        in1, in2, _, _ = way(c)
        exchange(1, c).wait_recv()
        here = cols(c)
        s2_ref[:, here] = (
            s1_ref[rows(in1 * quarter, quarter), here].astype(f32) + a_ref[:, here].astype(f32)
        ).astype(bf16)
        exchange(2, c).start()

    def step3(c):
        in1, in2, _, _ = way(c)
        exchange(2, c).wait_recv()
        here = cols(c)
        numerator = s2_ref[rows(in2 * eighth, eighth), here].astype(f32) + b_ref[:, here].astype(f32)
        mine = rows(core * half + in1 * quarter + in2 * eighth, eighth)
        total = wcol_ref[mine, :][:, 0:1]
        e_ref[mine, here] = (q_ref[mine, here] + expansion_weight * numerator / total).astype(bf16)
        exchange(3, c).start()

    def step4(c):
        exchange(3, c).wait_recv()
        exchange(4, c).start()

    def step5(c):
        exchange(4, c).wait_recv()
        exchange(5, c).start()

    def step0(c):
        here = cols(c)
        nb_ref[:, here] = jnp.dot(mix_ref[...], p_ref[:, here], preferred_element_type=f32).astype(bf16)
        exchange(0, c).start()

    def step6(c):
        exchange(5, c).wait_recv()
        here = cols(c)
        acc_ref[...] += dot_nt(e_ref[:, here], p_ref[:, here])

    def weights():
        for o in range(1, n_doc):
            ws_copy(o).wait_recv()
        total = ws_ref[0]
        for o in range(1, n_doc):
            total = total + ws_ref[o]
        column = jnp.sum(jnp.where(eye, total[0:1, :], 0.0), axis=1, keepdims=True)
        wcol_ref[...] = jnp.broadcast_to(column, wcol_ref.shape)

    body = (step0, step1, step2, step3, step4, step5, step6)
    for k, c in plan(chunks, queries * width * 2e-6):
        if (k, c) == (3, 0):
            weights()
        body[k](c)

    top = jnp.maximum(jnp.max(acc_ref[...], axis=1, keepdims=True), 1e-30)
    code_ref[...] = jnp.round(acc_ref[...] * (32767.0 / top)).astype(jnp.int32).astype(jnp.int16)
    for o in range(1, n_term):
        last_copy(o).start()
    top_ref[t] = jnp.broadcast_to(
        jnp.sum(jnp.where(eye, top, 0.0), axis=0, keepdims=True) / 32767.0, (8, queries)
    )
    for o in range(1, n_term):
        top_copy(o).start()

    for o in range(1, n_term):
        first_copy(o).wait_recv()
    total = first_ref[0]
    for s in range(1, n_term):
        total = total + first_ref[s]
    first_out[...] = total

    for o in range(1, n_term):
        fb_copy(o).wait_send()
        first_copy(o).wait_send()
    for o in range(1, n_doc):
        ws_copy(o).wait_send()

    def drain(c, carry):
        for step in range(6):
            exchange(step, c).wait_send()
        return carry

    lax.fori_loop(0, chunks, drain, 0)

    for o in range(1, n_term):
        top_copy(o).wait_recv()
    for s in range(n_term):
        column = jnp.sum(jnp.where(eye, top_ref[s][0:1, :], 0.0), axis=1, keepdims=True)
        wcol_ref[...] = jnp.broadcast_to(column, wcol_ref.shape)
        tops_ref[s] = wcol_ref[own_rows, :]
    total = acc_ref[own_rows, :]
    for o in range(1, n_term):
        last_copy(o).wait_recv()
        s = (t + n_term - o) % n_term
        steps = last_ref[s].astype(jnp.int32).astype(f32)
        total = total + steps * tops_ref[s][:, 0:1]
    final_out[...] = total

    for o in range(1, n_term):
        last_copy(o).wait_send()
        top_copy(o).wait_send()


def fused(postings, query_terms, query_levels, feedback_ids):
    docs, width = postings.shape
    queries, slots = query_terms.shape
    n_term, n_doc = lax.axis_size("term"), lax.axis_size("doc")
    chunks = next(c for c in (10, 6, 4, 2, 1) if width % (c * LANES) == 0)
    loads = next(c for c in (5, 3, 2, 1) if width % (c * LANES) == 0)
    rows_out = queries // n_term
    group = 8 * slots
    vmem = pltpu.VMEM
    dma = pltpu.SemaphoreType.DMA
    out = jax.ShapeDtypeStruct((rows_out, docs), f32)
    return pl.pallas_call(
        functools.partial(fused_kernel, n_term, n_doc, chunks, loads, slots),
        out_shape=(out, out),
        in_specs=[pl.BlockSpec(memory_space=pl.ANY), pl.BlockSpec(memory_space=pltpu.VMEM)],
        out_specs=(pl.BlockSpec(memory_space=pltpu.VMEM),) * 2,
        scratch_shapes=[
            vmem((docs, width), bf16),
            vmem((queries, width), f32),
            vmem((queries // 8, group), f32),
            vmem((queries // 8, group), f32),
            vmem((queries // 8, group), f32),
            vmem((queries, docs), f32),
            vmem((queries, docs), f32),
            vmem((queries, docs), bf16),
            vmem((n_term, 8, docs), f32),
            vmem((n_term, rows_out, docs), f32),
            vmem((n_doc, 8, queries), f32),
            vmem((queries, LANES), f32),
            vmem((queries, width), bf16),
            vmem((queries // 2, width), bf16),
            vmem((queries // 2, width), bf16),
            vmem((queries // 4, width), bf16),
            vmem((queries // 4, width), bf16),
            vmem((queries // 8, width), bf16),
            vmem((queries, width), bf16),
            vmem((queries, docs), f32),
            vmem((queries, docs), jnp.int16),
            vmem((n_term, rows_out, docs), jnp.int16),
            vmem((n_term, 8, queries), f32),
            vmem((n_term, rows_out, LANES), f32),
            dma((loads,)),
            dma((n_term - 1,)),
            dma((n_term - 1,)),
            dma((n_term - 1,)),
            dma((n_term - 1,)),
            dma((n_doc - 1,)),
            dma((n_doc - 1,)),
            dma((6, chunks)),
            dma((6, chunks)),
            dma((n_term - 1,)),
            dma((n_term - 1,)),
            dma((n_term - 1,)),
            dma((n_term - 1,)),
        ],
        compiler_params=pltpu.CompilerParams(
            collective_id=0, has_side_effects=True, vmem_limit_bytes=48 * 1024 * 1024
        ),
        cost_estimate=pl.CostEstimate(
            flops=6 * queries * docs * width, bytes_accessed=2 * docs * width, transcendentals=0
        ),
        name="fused_feedback",
    )(postings, jnp.concatenate([query_terms.T, query_levels.T, feedback_ids.T]))


def query_slice(query_terms, query_levels, width, offset):
    columns = offset + lax.iota(jnp.int32, width)

    def add_term(position, total):
        ids_now = lax.dynamic_index_in_dim(query_terms, position, 1, keepdims=True)
        weight_now = (
            lax.dynamic_index_in_dim(query_levels, position, 1, keepdims=True).astype(f32) / 100.0
        )
        return total + jnp.where(ids_now == columns[None, :], weight_now, 0.0)

    initial = jnp.zeros((query_terms.shape[0], width), f32)
    return lax.fori_loop(0, query_terms.shape[1], add_term, initial)


def general(postings, query_terms, query_levels, feedback_ids):
    doc_rows, width = postings.shape
    queries = query_terms.shape[0]
    group_rows = queries // lax.axis_size("term")
    term_index = lax.axis_index("term")
    doc_index = lax.axis_index("doc")
    query_part = query_slice(query_terms, query_levels, width, term_index * width)
    local_slot = feedback_ids - doc_index * doc_rows
    positions = lax.iota(jnp.int32, doc_rows)
    selector = (local_slot[:, :, None] == positions[None, None, :]).astype(f32)
    first_all = lax.psum(dot_nt(query_part.astype(bf16), postings), "term")
    first_scores = lax.dynamic_slice_in_dim(first_all, term_index * group_rows, group_rows, 0)
    feedback = jnp.sum(selector * first_all[:, None, :], axis=2).astype(bf16).astype(f32)
    mixing = jnp.sum(selector * feedback[:, :, None], axis=1).astype(bf16)
    numerator = jnp.dot(mixing, postings, preferred_element_type=f32)
    numerator, weight_sum = lax.psum((numerator, jnp.sum(feedback, axis=1)), "doc")
    expanded = (query_part + expansion_weight * numerator / weight_sum[:, None]).astype(bf16)
    final_scores = lax.psum_scatter(
        dot_nt(expanded, postings), "term", scatter_dimension=0, tiled=True
    )
    return first_scores, final_scores


def per_device(postings, query_terms, query_levels, feedback_ids):
    docs, width = postings.shape
    queries, slots = query_terms.shape
    fits = (
        lax.axis_size("doc") == 8
        and lax.axis_size("term") > 1
        and queries == LANES
        and queries % (16 * lax.axis_size("term")) == 0
        and width % BIN == 0
        and docs % LANES == 0
    )
    run = fused if fits else general
    return run(postings, query_terms, query_levels, feedback_ids)


def solution(mesh):
    return jax.shard_map(
        per_device,
        mesh=mesh,
        in_specs=(P("doc", "term"), P(), P(), P()),
        out_specs=(P("term", "doc"), P("term", "doc")),
        check_vma=False,
    )
```

```python
import functools

import jax
import jax.numpy as jnp
from jax import lax
from jax.experimental import pallas as pl
from jax.experimental.pallas import tpu as pltpu
from jax.sharding import PartitionSpec as P

expansion_weight = 0.25
MESH = pl.DeviceIdType.MESH
LANES = 128
BIN = 256
NT = (((1,), (1,)), ((), ()))
f32 = jnp.float32
bf16 = jnp.bfloat16


def dot_nt(a, b):
    return lax.dot_general(a, b, NT, preferred_element_type=f32)


def plan(chunks, mega):
    part = mega / chunks
    send = (part * 0.83, part * 5.0, part * 2.5, part * 2.5, part * 5.0, part * 0.83)
    work = (3.0 / chunks, 1.0 / chunks, 0.5 / chunks, 1.0 / chunks, 0.02, 0.02, 4.0 / chunks)
    free = {"twin": 0.0, "x": 0.0, "y": 0.0}
    arrival, at, order = {}, [0] * 7, []
    now = 0.0
    rank = (5, 4, 3, 2, 1, 0, 6)

    def due(k):
        return 0.0 if k == 0 else arrival.get((k - 1, at[k]), float("inf"))

    while at[6] < chunks:
        open_steps = [k for k in rank if at[k] < chunks]
        ready = [k for k in open_steps if due(k) <= now]
        k = ready[0] if ready else min(open_steps, key=due)
        c = at[k]
        now = max(now, due(k)) + work[k]
        if k < 6:
            link = "twin" if k in (0, 5) else "xy"[(c + (k in (2, 3))) % 2]
            free[link] = max(now, free[link]) + send[k]
            arrival[k, c] = free[link] + 1.0
        at[k] += 1
        order.append((k, c))
    return order


def fused_kernel(
    n_term, n_doc, chunks, loads,
    slots, postings, small, first_out, final_out,
    p_ref, q_ref, hi_ref, lo_ref, lev_ref, part_ref, sel_ref, mix_ref,
    fb_ref, first_ref, ws_ref, wcol_ref, nb_ref, tw_ref, s1_ref, a_ref, s2_ref, b_ref,
    e_ref, acc_ref, code_ref, last_ref, top_ref, tops_ref,
    p_sem, fb_send, fb_recv, first_send, first_recv, ws_send, ws_recv,
    pipe_send, pipe_recv, last_send, last_recv, top_send, top_recv,
):
    t = lax.axis_index("term")
    d = lax.axis_index("doc")
    docs, width = p_ref.shape
    queries = small.shape[1]
    cw = width // chunks
    lw = width // loads
    his = width // BIN
    rows_out = queries // n_term
    half, quarter, eighth = queries // 2, queries // 4, queries // 8

    core = d % 2
    bit1 = (d // 2) % 2
    bit2 = (d // 4) % 2

    def cols(c):
        return pl.ds(pl.multiple_of(c * cw, LANES), cw)

    def load_cols(c):
        return pl.ds(pl.multiple_of(c * lw, LANES), lw)

    def load(c):
        here = load_cols(c)
        return pltpu.make_async_copy(postings.at[:, here], p_ref.at[:, here], p_sem.at[c])

    for c in range(loads):
        load(c).start()

    barrier = pltpu.get_barrier_semaphore()
    for o in range(1, n_term):
        pl.semaphore_signal(barrier, inc=1, device_id={"term": (t + o) % n_term}, device_id_type=MESH)
    for o in range(1, n_doc):
        pl.semaphore_signal(barrier, inc=1, device_id={"doc": (d + o) % n_doc}, device_id_type=MESH)

    group = 8 * slots
    spread = (
        lax.broadcasted_iota(jnp.int32, (slots, group), 0)
        == lax.broadcasted_iota(jnp.int32, (slots, group), 1) % slots
    ).astype(bf16)
    own = (
        lax.broadcasted_iota(jnp.int32, (queries, group), 0) % 8
        == lax.broadcasted_iota(jnp.int32, (queries, group), 1) // slots
    )

    def lay(values):
        wide = lax.dot_general(
            values.astype(f32).astype(bf16), spread, (((0,), (0,)), ((), ())), preferred_element_type=f32
        )
        return jnp.sum(jnp.where(own, wide, 0.0).reshape(queries // 8, 8, group), axis=1)

    ids_now = small[:slots]
    q8 = (lax.broadcasted_iota(jnp.int32, (queries // 8, group), 1) // slots).astype(f32)
    hi = lay(ids_now // BIN) - (t * his).astype(f32)
    hi_ref[...] = hi * 8.0 + q8
    lo_ref[...] = lay(ids_now % BIN)
    lev_ref[...] = lay(small[slots : 2 * slots])

    row_code = lax.broadcasted_iota(jnp.int32, (his * 8, group), 0).astype(f32)
    lane_code = lax.broadcasted_iota(jnp.int32, (BIN, group), 0).astype(f32)

    def build_one(g):
        left = jnp.where(
            hi_ref[pl.ds(g, 1), :] == row_code, lev_ref[pl.ds(g, 1), :], 0.0
        ).astype(bf16)
        right = jnp.where(lo_ref[pl.ds(g, 1), :] == lane_code, 1.0, 0.0).astype(bf16)
        block = dot_nt(left, right) * 0.01
        rows = pl.ds(pl.multiple_of(g * 8, 8), 8)
        for h in range(his):
            q_ref[rows, h * BIN : (h + 1) * BIN] = block[h * 8 : (h + 1) * 8]

    def build(g, carry):
        for i in range(4):
            build_one(g * 4 + i)
        return carry

    lax.fori_loop(0, queries // 32, build, 0)

    place = lax.broadcasted_iota(jnp.int32, (queries, docs), 1)
    local = small[2 * slots :].T - d * docs
    sel = place == local[:, 0:1]
    for j in range(1, local.shape[1]):
        sel = sel | (place == local[:, j : j + 1])
    sel_ref[...] = jnp.where(sel, 1.0, 0.0)

    part_ref[...] = jnp.zeros_like(part_ref)

    def score(c, carry):
        load(c).wait()
        part_ref[...] += dot_nt(q_ref[:, load_cols(c)].astype(bf16), p_ref[:, load_cols(c)])
        return carry

    lax.fori_loop(0, loads, score, 0)

    pl.semaphore_wait(barrier, n_term + n_doc - 2)

    fb_ref[t] = jnp.sum((sel_ref[...] * part_ref[...]).reshape(queries // 8, 8, docs), axis=0)

    def fb_copy(o):
        return pltpu.make_async_remote_copy(
            fb_ref.at[t], fb_ref.at[t], fb_send.at[o - 1], fb_recv.at[o - 1],
            device_id={"term": (t + o) % n_term}, device_id_type=MESH,
        )

    def first_copy(o):
        peer = (t + o) % n_term
        return pltpu.make_async_remote_copy(
            part_ref.at[pl.ds(pl.multiple_of(peer * rows_out, 8), rows_out), :], first_ref.at[t],
            first_send.at[o - 1], first_recv.at[o - 1],
            device_id={"term": peer}, device_id_type=MESH,
        )

    def last_copy(o):
        peer = (t + o) % n_term
        return pltpu.make_async_remote_copy(
            code_ref.at[pl.ds(pl.multiple_of(peer * rows_out, 16), rows_out), :], last_ref.at[t],
            last_send.at[o - 1], last_recv.at[o - 1],
            device_id={"term": peer}, device_id_type=MESH,
        )

    def top_copy(o):
        return pltpu.make_async_remote_copy(
            top_ref.at[t], top_ref.at[t], top_send.at[o - 1], top_recv.at[o - 1],
            device_id={"term": (t + o) % n_term}, device_id_type=MESH,
        )

    def ws_copy(o):
        return pltpu.make_async_remote_copy(
            ws_ref.at[d], ws_ref.at[d], ws_send.at[o - 1], ws_recv.at[o - 1],
            device_id={"doc": (d + o) % n_doc}, device_id_type=MESH,
        )

    for o in range(1, n_term):
        fb_copy(o).start()
    for o in range(1, n_term):
        first_copy(o).start()
    own_rows = pl.ds(pl.multiple_of(t * rows_out, 8), rows_out)
    first_ref[t] = part_ref[own_rows, :]
    for o in range(1, n_term):
        fb_copy(o).wait_recv()
    fb_sum = fb_ref[0]
    for s in range(1, n_term):
        fb_sum = fb_sum + fb_ref[s]
    fb_row = jnp.sum(fb_sum, axis=0, keepdims=True)
    mix_ref[...] = (sel_ref[...] * fb_row).astype(bf16)

    ones = jnp.ones((16, docs), bf16)
    ws_ref[d] = dot_nt(ones, mix_ref[...])[:8]
    for o in range(1, n_doc):
        ws_copy(o).start()

    def copy_of(step, c, src, dst, peer):
        return pltpu.make_async_remote_copy(
            src, dst, pipe_send.at[step, c], pipe_recv.at[step, c],
            device_id={"doc": peer}, device_id_type=MESH,
        )

    twin = d + 1 - 2 * core

    def way(c):
        odd = c % 2
        even = 1 - odd
        in1 = even * bit1 + odd * bit2
        in2 = even * bit2 + odd * bit1
        peer1 = d + (even * 2 + odd * 4) * (1 - 2 * in1)
        peer2 = d + (even * 4 + odd * 2) * (1 - 2 * in2)
        return in1, in2, peer1, peer2

    def rows(start, size):
        return pl.ds(pl.multiple_of(start, 16), size)

    def exchange(step, c):
        in1, in2, peer1, peer2 = way(c)
        here = cols(c)
        if step == 0:
            return copy_of(0, c, nb_ref.at[rows((1 - core) * half, half), here], tw_ref.at[:, here], twin)
        if step == 1:
            return copy_of(1, c, s1_ref.at[rows((1 - in1) * quarter, quarter), here], a_ref.at[:, here], peer1)
        if step == 2:
            return copy_of(2, c, s2_ref.at[rows((1 - in2) * eighth, eighth), here], b_ref.at[:, here], peer2)
        base = core * half
        if step == 3:
            at = e_ref.at[rows(base + in1 * quarter + in2 * eighth, eighth), here]
            return copy_of(3, c, at, at, peer2)
        if step == 4:
            at = e_ref.at[rows(base + in1 * quarter, quarter), here]
            return copy_of(4, c, at, at, peer1)
        at = e_ref.at[rows(base, half), here]
        return copy_of(5, c, at, at, twin)

    acc_ref[...] = jnp.zeros_like(acc_ref)
    eye = (
        lax.broadcasted_iota(jnp.int32, (queries, queries), 0)
        == lax.broadcasted_iota(jnp.int32, (queries, queries), 1)
    )

    def step1(c):
        exchange(0, c).wait_recv()
        here = cols(c)
        s1_ref[:, here] = (
            nb_ref[rows(core * half, half), here].astype(f32) + tw_ref[:, here].astype(f32)
        ).astype(bf16)
        exchange(1, c).start()

    def step2(c):
        in1, in2, _, _ = way(c)
        exchange(1, c).wait_recv()
        here = cols(c)
        s2_ref[:, here] = (
            s1_ref[rows(in1 * quarter, quarter), here].astype(f32) + a_ref[:, here].astype(f32)
        ).astype(bf16)
        exchange(2, c).start()

    def step3(c):
        in1, in2, _, _ = way(c)
        exchange(2, c).wait_recv()
        here = cols(c)
        numerator = s2_ref[rows(in2 * eighth, eighth), here].astype(f32) + b_ref[:, here].astype(f32)
        mine = rows(core * half + in1 * quarter + in2 * eighth, eighth)
        total = wcol_ref[mine, :][:, 0:1]
        e_ref[mine, here] = (q_ref[mine, here] + expansion_weight * numerator / total).astype(bf16)
        exchange(3, c).start()

    def step4(c):
        exchange(3, c).wait_recv()
        exchange(4, c).start()

    def step5(c):
        exchange(4, c).wait_recv()
        exchange(5, c).start()

    def step0(c):
        here = cols(c)
        nb_ref[:, here] = jnp.dot(mix_ref[...], p_ref[:, here], preferred_element_type=f32).astype(bf16)
        exchange(0, c).start()

    def step6(c):
        exchange(5, c).wait_recv()
        here = cols(c)
        acc_ref[...] += dot_nt(e_ref[:, here], p_ref[:, here])

    def weights():
        for o in range(1, n_doc):
            ws_copy(o).wait_recv()
        total = ws_ref[0]
        for o in range(1, n_doc):
            total = total + ws_ref[o]
        column = jnp.sum(jnp.where(eye, total[0:1, :], 0.0), axis=1, keepdims=True)
        wcol_ref[...] = jnp.broadcast_to(column, wcol_ref.shape)

    body = (step0, step1, step2, step3, step4, step5, step6)
    for k, c in plan(chunks, queries * width * 2e-6):
        if (k, c) == (3, 0):
            weights()
        body[k](c)

    top = jnp.maximum(jnp.max(acc_ref[...], axis=1, keepdims=True), 1e-30)
    code_ref[...] = jnp.round(acc_ref[...] * (32767.0 / top)).astype(jnp.int32).astype(jnp.int16)
    for o in range(1, n_term):
        last_copy(o).start()
    top_ref[t] = jnp.broadcast_to(
        jnp.sum(jnp.where(eye, top, 0.0), axis=0, keepdims=True) / 32767.0, (8, queries)
    )
    for o in range(1, n_term):
        top_copy(o).start()

    for o in range(1, n_term):
        first_copy(o).wait_recv()
    total = first_ref[0]
    for s in range(1, n_term):
        total = total + first_ref[s]
    first_out[...] = total

    for o in range(1, n_term):
        fb_copy(o).wait_send()
        first_copy(o).wait_send()
    for o in range(1, n_doc):
        ws_copy(o).wait_send()

    def drain(c, carry):
        for step in range(6):
            exchange(step, c).wait_send()
        return carry

    lax.fori_loop(0, chunks, drain, 0)

    for o in range(1, n_term):
        top_copy(o).wait_recv()
    for s in range(n_term):
        column = jnp.sum(jnp.where(eye, top_ref[s][0:1, :], 0.0), axis=1, keepdims=True)
        wcol_ref[...] = jnp.broadcast_to(column, wcol_ref.shape)
        tops_ref[s] = wcol_ref[own_rows, :]
    total = acc_ref[own_rows, :]
    for o in range(1, n_term):
        last_copy(o).wait_recv()
        s = (t + n_term - o) % n_term
        steps = last_ref[s].astype(jnp.int32).astype(f32)
        total = total + steps * tops_ref[s][:, 0:1]
    final_out[...] = total

    for o in range(1, n_term):
        last_copy(o).wait_send()
        top_copy(o).wait_send()


def fused(postings, query_terms, query_levels, feedback_ids):
    docs, width = postings.shape
    queries, slots = query_terms.shape
    n_term, n_doc = lax.axis_size("term"), lax.axis_size("doc")
    chunks = next(c for c in (6, 4, 2, 1) if width % (c * LANES) == 0)
    loads = next(c for c in (5, 3, 2, 1) if width % (c * LANES) == 0)
    rows_out = queries // n_term
    group = 8 * slots
    vmem = pltpu.VMEM
    dma = pltpu.SemaphoreType.DMA
    out = jax.ShapeDtypeStruct((rows_out, docs), f32)
    return pl.pallas_call(
        functools.partial(fused_kernel, n_term, n_doc, chunks, loads, slots),
        out_shape=(out, out),
        in_specs=[pl.BlockSpec(memory_space=pl.ANY), pl.BlockSpec(memory_space=pltpu.VMEM)],
        out_specs=(pl.BlockSpec(memory_space=pltpu.VMEM),) * 2,
        scratch_shapes=[
            vmem((docs, width), bf16),
            vmem((queries, width), f32),
            vmem((queries // 8, group), f32),
            vmem((queries // 8, group), f32),
            vmem((queries // 8, group), f32),
            vmem((queries, docs), f32),
            vmem((queries, docs), f32),
            vmem((queries, docs), bf16),
            vmem((n_term, 8, docs), f32),
            vmem((n_term, rows_out, docs), f32),
            vmem((n_doc, 8, queries), f32),
            vmem((queries, LANES), f32),
            vmem((queries, width), bf16),
            vmem((queries // 2, width), bf16),
            vmem((queries // 2, width), bf16),
            vmem((queries // 4, width), bf16),
            vmem((queries // 4, width), bf16),
            vmem((queries // 8, width), bf16),
            vmem((queries, width), bf16),
            vmem((queries, docs), f32),
            vmem((queries, docs), jnp.int16),
            vmem((n_term, rows_out, docs), jnp.int16),
            vmem((n_term, 8, queries), f32),
            vmem((n_term, rows_out, LANES), f32),
            dma((loads,)),
            dma((n_term - 1,)),
            dma((n_term - 1,)),
            dma((n_term - 1,)),
            dma((n_term - 1,)),
            dma((n_doc - 1,)),
            dma((n_doc - 1,)),
            dma((6, chunks)),
            dma((6, chunks)),
            dma((n_term - 1,)),
            dma((n_term - 1,)),
            dma((n_term - 1,)),
            dma((n_term - 1,)),
        ],
        compiler_params=pltpu.CompilerParams(
            collective_id=0, has_side_effects=True, vmem_limit_bytes=48 * 1024 * 1024
        ),
        cost_estimate=pl.CostEstimate(
            flops=6 * queries * docs * width, bytes_accessed=2 * docs * width, transcendentals=0
        ),
        name="fused_feedback",
    )(postings, jnp.concatenate([query_terms.T, query_levels.T, feedback_ids.T]))


def query_slice(query_terms, query_levels, width, offset):
    columns = offset + lax.iota(jnp.int32, width)

    def add_term(position, total):
        ids_now = lax.dynamic_index_in_dim(query_terms, position, 1, keepdims=True)
        weight_now = (
            lax.dynamic_index_in_dim(query_levels, position, 1, keepdims=True).astype(f32) / 100.0
        )
        return total + jnp.where(ids_now == columns[None, :], weight_now, 0.0)

    initial = jnp.zeros((query_terms.shape[0], width), f32)
    return lax.fori_loop(0, query_terms.shape[1], add_term, initial)


def general(postings, query_terms, query_levels, feedback_ids):
    doc_rows, width = postings.shape
    queries = query_terms.shape[0]
    group_rows = queries // lax.axis_size("term")
    term_index = lax.axis_index("term")
    doc_index = lax.axis_index("doc")
    query_part = query_slice(query_terms, query_levels, width, term_index * width)
    local_slot = feedback_ids - doc_index * doc_rows
    positions = lax.iota(jnp.int32, doc_rows)
    selector = (local_slot[:, :, None] == positions[None, None, :]).astype(f32)
    first_all = lax.psum(dot_nt(query_part.astype(bf16), postings), "term")
    first_scores = lax.dynamic_slice_in_dim(first_all, term_index * group_rows, group_rows, 0)
    feedback = jnp.sum(selector * first_all[:, None, :], axis=2).astype(bf16).astype(f32)
    mixing = jnp.sum(selector * feedback[:, :, None], axis=1).astype(bf16)
    numerator = jnp.dot(mixing, postings, preferred_element_type=f32)
    numerator, weight_sum = lax.psum((numerator, jnp.sum(feedback, axis=1)), "doc")
    expanded = (query_part + expansion_weight * numerator / weight_sum[:, None]).astype(bf16)
    final_scores = lax.psum_scatter(
        dot_nt(expanded, postings), "term", scatter_dimension=0, tiled=True
    )
    return first_scores, final_scores


def per_device(postings, query_terms, query_levels, feedback_ids):
    docs, width = postings.shape
    queries, slots = query_terms.shape
    fits = (
        lax.axis_size("doc") == 8
        and lax.axis_size("term") > 1
        and queries == LANES
        and queries % (16 * lax.axis_size("term")) == 0
        and width % BIN == 0
        and docs % LANES == 0
    )
    run = fused if fits else general
    return run(postings, query_terms, query_levels, feedback_ids)


def solution(mesh):
    return jax.shard_map(
        per_device,
        mesh=mesh,
        in_specs=(P("doc", "term"), P(), P(), P()),
        out_specs=(P("term", "doc"), P("term", "doc")),
        check_vma=False,
    )
```
